256 devices in a mesh: grp: 8 (over x, core), seg: 32 (over z, y).
Axes of the slice: x: 4, y: 4, z: 8, core: 2. Of those that a mesh axis runs over, the one named last changes fastest.
Arguments:
- frames: bfloat16 [2048, 64, 192], P(('grp', 'seg')), may hold values from -6 to 6
- conv_first: bfloat16 [4, 4, 3, 64], replicated, may hold values from -0.875 to 0.875
- second_kernel_weight: bfloat16 [4, 4, 64, 128], replicated, may hold values from -0.25 to 0.25
- conv_third: bfloat16 [4, 4, 128, 256], replicated, may hold values from -0.1875 to 0.1875
- observe_map: bfloat16 [256, 256], replicated, may hold values from -0.375 to 0.375
- skew_source: float32 [256, 256], replicated, may hold values from -0.375 to 0.375
- retain: float32 [2048, 256], P(('grp', 'seg')), may hold values from 0 to 1
Outputs:
- filtered: float32 [2048, 256], P(('grp', 'seg'))
The draws below stay inside these ranges and needn't reach their ends.
All inputs are finite; a program needn't handle non-finite values.
Results may differ from the reference program's by a relative error of at most 0.004.
Values sent between devices are 32-bit elements; how exact they have to be, the bound alone decides.
No kernel may reach another device: no remote copies, remote signals or barrier semaphores. Data moves between devices by JAX's collectives and lax.ppermute only.
A program may use at most 192 MiB of HBM per device.

```python
import jax
import jax.numpy as jnp
from jax import lax

LATENT_DIM = 256
CH_FIRST = 64
CH_SECOND = 128
IMG = 64
TAYLOR = 8
FRAMES_DEV = 8
SPAN_PICTURES = 2048


def draw_retain(key, part):
    noise_seeds = jax.random.split(jax.random.fold_in(key, 17), 5)
    share = 0.5
    slow = jax.random.bernoulli(noise_seeds[0], share, (LATENT_DIM,))
    slow_rate = jnp.exp(jax.random.uniform(noise_seeds[1], (LATENT_DIM,), jnp.float32, jnp.log(0.1 / SPAN_PICTURES), jnp.log(1.0 / SPAN_PICTURES)))
    quick_speed = jnp.exp(jax.random.uniform(noise_seeds[2], (LATENT_DIM,), jnp.float32, jnp.log(1.0 / 50.0), jnp.log(1.0 / 30.0)))
    rate = jnp.where(slow, slow_rate, quick_speed)
    jitter = jnp.exp(jax.random.uniform(noise_seeds[3], (SPAN_PICTURES, LATENT_DIM), jnp.float32, jnp.log(0.5), jnp.log(2.0)))
    picture_group_run = jax.random.bernoulli(noise_seeds[4], 4.0 / SPAN_PICTURES, (SPAN_PICTURES, 1))
    update_multiplier = jnp.where(picture_group_run, 0.65, 1.0)
    return (jnp.exp(-rate[None, :] * jitter) * update_multiplier).astype(jnp.float32)


def levels(stream_key, dims, cuts, least, largest):
    loudness, own = 1.0, jax.random.fold_in(stream_key, 6)
    for position, blocks in cuts:
        heights = jnp.exp(jax.random.uniform(jax.random.fold_in(own, position), (blocks,), jnp.float32, least / len(cuts), largest / len(cuts)))
        loudness = loudness * jnp.repeat(heights, dims[position] // blocks).reshape([-1 if axis == position else 1 for axis in range(len(dims))])
    return loudness


def bell_draw(stream_key, shape, spread, limit, pieces=(), kind=jnp.bfloat16):
    factor_of = levels(stream_key, shape, pieces, -0.22, 0.18) if pieces else 1.0
    result = jax.random.normal(stream_key, shape, jnp.float32) * spread * factor_of
    return jnp.minimum(jnp.maximum(result, -limit), limit).astype(kind)


def setup_inputs(seed: int = 0) -> dict:
    seeds = jax.random.split(jax.random.key(seed), 8)
    return {
        "frames": bell_draw(seeds[0], (SPAN_PICTURES, IMG, 3 * IMG), 1.0, 6.0, ((0, 256),)),
        "conv_first": bell_draw(seeds[1], (4, 4, 3, CH_FIRST), 48 ** -0.5, 0.875),
        "second_kernel_weight": bell_draw(seeds[2], (4, 4, CH_FIRST, CH_SECOND), (8 * CH_FIRST) ** -0.5, 0.25),
        "conv_third": bell_draw(seeds[3], (4, 4, CH_SECOND, LATENT_DIM), (8 * CH_SECOND) ** -0.5, 0.1875),
        "observe_map": bell_draw(seeds[4], (LATENT_DIM, LATENT_DIM), LATENT_DIM ** -0.5, 0.375),
        "skew_source": bell_draw(seeds[5], (LATENT_DIM, LATENT_DIM), LATENT_DIM ** -0.5, 0.375, (), jnp.float32),
        "retain": draw_retain(jax.random.fold_in(seeds[7], 71), 0),
    }


def make_rotation(skew_source, total_frames):
    skew = (skew_source - skew_source.T) * (0.7 / jnp.sqrt(jnp.float32(total_frames)))
    eye_matrix = jnp.eye(skew.shape[0], dtype=jnp.float32)
    term = eye_matrix
    total = eye_matrix
    for order in range(1, TAYLOR + 1):
        term = jnp.dot(term, skew, precision=lax.Precision.HIGHEST) / order
        total = total + term
    return total

def apply_convolution(inputs, kernel):
    return lax.conv_general_dilated(inputs, kernel, (2, 2), ((1, 1), (1, 1)), dimension_numbers=('NHWC', 'HWIO', 'NHWC'), preferred_element_type=jnp.float32)

def encode(frames, conv_first, second_kernel_weight, conv_third):
    count = frames.shape[0]
    pixels = frames.reshape(count, frames.shape[1], frames.shape[1], 3)
    first = jax.nn.relu(apply_convolution(pixels, conv_first)).astype(jnp.bfloat16)
    second = jax.nn.relu(apply_convolution(first, second_kernel_weight)).astype(jnp.bfloat16)
    third = jax.nn.relu(apply_convolution(second, conv_third))
    return lax.optimization_barrier(jnp.mean(third, axis=(1, 2))).astype(jnp.bfloat16)

def reference(frames, conv_first, second_kernel_weight, conv_third, observe_map, skew_source, retain):
    rotation = make_rotation(skew_source, SPAN_PICTURES)
    blocks = frames.reshape(SPAN_PICTURES // FRAMES_DEV, FRAMES_DEV, frames.shape[1], frames.shape[2])
    pooled = lax.map(lambda block: encode(block, conv_first, second_kernel_weight, conv_third), blocks)
    pooled = pooled.reshape(SPAN_PICTURES, -1)
    drive = (1.0 - retain) * jnp.dot(pooled, observe_map, preferred_element_type=jnp.float32)

    def advance(state, inputs):
        keep, push = inputs
        state = keep * jnp.dot(rotation, state, precision=lax.Precision.HIGHEST) + push
        return (state, state)
    start = jnp.zeros((retain.shape[1],), jnp.float32)
    final, filtered = lax.scan(advance, start, (retain, drive))
    return filtered
```

```python
import functools

import jax
import jax.numpy as jnp
import numpy as np
from jax import lax
from jax.experimental import pallas as pl
from jax.experimental.pallas import tpu as pltpu
from jax.sharding import Mesh, PartitionSpec as P

VMEM = pl.BlockSpec(memory_space=pltpu.VMEM)
LIMIT = 40 * 1024 * 1024
F32, BF16 = jnp.float32, jnp.bfloat16


def halves(value):
    top = value.astype(BF16)
    return top, (value - top.astype(F32)).astype(BF16)


def dot3(left, right):
    (left_top, left_rest), (right_top, right_rest) = left, right
    return (
        jnp.dot(left_top, right_rest, preferred_element_type=F32)
        + jnp.dot(left_rest, right_top, preferred_element_type=F32)
    ) + jnp.dot(left_top, right_top, preferred_element_type=F32)


def product(left, right):
    return dot3(halves(left), halves(right))


def call(kernel, outs, scratch, flops, traffic, *args):
    return pl.pallas_call(
        kernel,
        out_shape=[jax.ShapeDtypeStruct(shape, kind) for shape, kind in outs],
        in_specs=[VMEM] * len(args),
        out_specs=[VMEM] * len(outs),
        scratch_shapes=[pltpu.VMEM(shape, kind) for shape, kind in scratch],
        compiler_params=pltpu.CompilerParams(vmem_limit_bytes=LIMIT),
        cost_estimate=pl.CostEstimate(flops=flops, bytes_accessed=traffic, transcendentals=0),
    )(*args)


def rows_of(store, step, first, length):
    ways = store.shape[0]
    pieces = []
    for turn in range(ways // step):
        row = first + step * turn
        pieces.append(store[row % ways, pl.ds(row // ways, length * step // ways)])
    return pieces


def put_rows(store, value, first, start, size):
    ways = store.shape[0]
    share = value.shape[0] // ways
    for turn in range(ways):
        row = first + turn
        store[row % ways, pl.ds(row // ways, share), :, start : start + size] = value[turn * share : (turn + 1) * share]


def clear_rows(store, rows):
    for row in rows:
        store[row % store.shape[0], row // store.shape[0]] = jnp.zeros(store.shape[2:], F32)


def flatten(pieces, start, size):
    return jnp.concatenate([p[:, :, start : start + size].reshape(-1, size) for p in pieces], 0).astype(BF16)


def encoder_kernel(frames, band, second, third, observe, retain, drive, flat, lines, wide, one, two):
    count, height, row = frames.shape
    lanes = lines.shape[3]
    pixels = frames[...].astype(F32).reshape(count * height, row)
    pixels = jnp.concatenate([pixels, jnp.zeros((count * height, lanes - row), F32)], 1)
    pixels = pltpu.roll(pixels, 9, 1)
    flat[0] = pixels[:, :128]
    flat[1] = pixels[:, 128:]
    clear_rows(lines, (0, height + 1))
    for h in range(height):
        for side in range(2):
            picked = flat[side, pl.ds(h, count, stride=height), :]
            lines[(h + 1) % 8, (h + 1) // 8, :, 128 * side : 128 * side + 128] = picked
    taps, depth, broad = band.shape
    room = lanes - depth
    wide[...] = jnp.zeros_like(wide)
    for tap in range(taps):
        wide[tap, room : room + depth, :] = band[tap]

    rows = height // 2
    clear_rows(one, (0, rows + 1))
    sources = [flatten(rows_of(lines, 2, tap, rows), 0, lanes) for tap in range(taps)]
    total = one.shape[3]
    for start in range(0, total, broad):
        size = min(broad, total - start)
        shift = start // broad * 48
        value = jnp.zeros((rows * count, size), F32)
        for tap in range(taps):
            weights = wide[tap, room - shift : room - shift + lanes, :size]
            value += jnp.dot(sources[tap], weights, preferred_element_type=F32)
        value = jnp.maximum(value, 0.0).astype(BF16).astype(F32)
        lane = lax.broadcasted_iota(jnp.int32, value.shape, 1) + start
        if start == 0:
            value = jnp.where(lane >= 64, value, 0.0)
        if start + size == total:
            value = jnp.where(lane < total - 64, value, 0.0)
        put_rows(one, value.reshape(rows, count, size), 1, start, size)

    rows = rows // 2
    clear_rows(two, (0, rows + 1))
    edge = jnp.zeros(two.shape[:3] + (128,), F32)
    two[:, :, :, :128] = edge
    two[:, :, :, two.shape[3] - 128 :] = edge
    group = 4
    for left in range(0, rows, group):
        value = jnp.zeros((group * rows * count, 128), F32)
        for tap in range(4):
            pieces = []
            for j in range(left, left + group):
                pieces.append(flatten([p[:, :, 128 * j : 128 * j + 256] for p in rows_of(one, 2, tap, rows)], 0, 256))
            value += jnp.dot(jnp.concatenate(pieces, 0), second[tap], preferred_element_type=F32)
        value = jnp.maximum(value, 0.0).astype(BF16).astype(F32).reshape(group, rows, count, 128)
        for k in range(group):
            put_rows(two, value[k], 1, 128 * (left + k + 1), 128)

    rows = rows // 2
    value = jnp.zeros((rows * rows * count, third.shape[2]), F32)
    for tap in range(4):
        pieces = [flatten(rows_of(two, 2, tap, rows), 256 * j, 512) for j in range(rows)]
        value += jnp.dot(jnp.concatenate(pieces, 0), third[tap], preferred_element_type=F32)
    value = jnp.maximum(value, 0.0).reshape(rows * rows, count, value.shape[1])
    pooled = (jnp.sum(value, 0) * (1.0 / (rows * rows))).astype(BF16)
    drive[...] = (1.0 - retain[...]) * jnp.dot(pooled, observe[...], preferred_element_type=F32)


def encode(frames, conv_first, second_kernel_weight, conv_third, observe_map, retain):
    count, height, row = frames.shape
    taps = conv_first.reshape(4, 12, 64)
    band = jnp.stack([jnp.pad(taps, ((0, 0), (6 * k, 52 - 6 * k), (0, 0))) for k in range(8)], 2).reshape(4, 64, 512)
    (drive,) = call(
        encoder_kernel,
        [(retain.shape, F32)],
        [
            ((2, count * height, 128), F32),
            ((8, height // 8 + 1, count, 256), F32),
            ((4, 448, 512), BF16),
            ((4, height // 8 + 1, count, 34 * 64), F32),
            ((2, height // 8 + 1, count, 18 * 128), F32),
        ],
        4 * 10**9,
        4 * 10**6,
        frames,
        band,
        second_kernel_weight.reshape(4, 256, 128),
        conv_third.reshape(4, 512, 256),
        observe_map,
        retain,
    )
    return drive


def order(pieces, place):
    count = len(pieces)
    me = lax.axis_index("y")
    for shift, piece in enumerate(pieces):
        slot = lax.rem(me - shift + count, count)
        place[pl.ds(slot, 1)] = piece[...][None]


def turn_kernel(factor, source, top, rest):
    width = source.shape[0]
    skew = (source[...].T - source[...]) * factor
    first = halves(skew)
    two = dot3(first, first)
    square = halves(two)
    three = dot3(first, square)
    four = dot3(square, square)
    row = lax.broadcasted_iota(jnp.int32, (width, width), 0)
    eye = (row == lax.broadcasted_iota(jnp.int32, (width, width), 1)).astype(F32)
    upper = eye / 24.0 + skew / 120.0 + two / 720.0 + three / 5040.0 + four / 40320.0
    turn = skew + two / 2.0 + three / 6.0 + product(four, upper)
    top[...], rest[...] = halves(turn)


def maps_kernel(top, rest, *refs):
    pieces, (maps, block, own, keeps) = refs[:-4], refs[-4:]
    count = len(pieces)
    order(pieces, keeps)
    local, width = pieces[0].shape
    turn = (top[...], rest[...])
    row = lax.broadcasted_iota(jnp.int32, (width, width), 0)
    eye = (row == lax.broadcasted_iota(jnp.int32, (width, width), 1)).astype(F32)
    start = eye + (turn[0].astype(F32) + turn[1].astype(F32))
    values = [start * keeps[b, 0:1, :] for b in range(count)]
    for step in range(1, local):
        values = [(v + dot3(halves(v), turn)) * keeps[b, step : step + 1, :] for b, v in enumerate(values)]
    for b in range(count):
        maps[b] = values[b]
    me = lax.axis_index("y")
    before, mine = values[0], eye
    for b in range(1, count):
        mine = jnp.where(me == b, before, mine)
        before = product(before, values[b])
    own[...] = mine
    block[...] = before


def local_kernel(top, rest, maps, *refs):
    count = maps.shape[0]
    keep_pieces, push_pieces = refs[:count], refs[count : 2 * count]
    end, entry, keeps, pushes = refs[2 * count :]
    order(keep_pieces, keeps)
    order(push_pieces, pushes)
    turn = (top[...], rest[...])
    state = jnp.concatenate([pushes[b, 0:1, :] for b in range(count)] * 2, 0)
    for step in range(1, keeps.shape[1]):
        keep = jnp.concatenate([keeps[b, step : step + 1, :] for b in range(count)] * 2, 0)
        push = jnp.concatenate([pushes[b, step : step + 1, :] for b in range(count)] * 2, 0)
        state = (state + dot3(halves(state), turn)) * keep + push
    me = lax.axis_index("y")
    width = state.shape[1]
    spread = lambda b: jnp.broadcast_to(state[b : b + 1], (8, width))
    before, mine = spread(0), jnp.zeros((8, width), F32)
    for b in range(1, count):
        mine = jnp.where(me == b, before, mine)
        before = product(before, maps[b]) + spread(b)
    end[...] = before
    entry[...] = mine


def final_kernel(top, rest, entry, own_map, own_entry, retain, drive, out):
    turn = (top[...], rest[...])
    state = product(entry[...], own_map[...]) + own_entry[...]
    rows = []
    for step in range(retain.shape[0]):
        state = (state + dot3(halves(state), turn)) * retain[step : step + 1, :] + drive[step : step + 1, :]
        rows.append(state[0:1])
    out[...] = jnp.concatenate(rows, 0)


def dot(a, b):
    return jnp.dot(a, b, precision=lax.Precision.HIGH, preferred_element_type=F32)


def around(value, axis, count):
    return [value] + [lax.ppermute(value, axis, [(i, (i + k) % count) for i in range(count)]) for k in range(1, count)]


def exchange_pairs(bit, count):
    if 2 * bit == count:
        return [(i, count - 1 - i) for i in range(count)]
    return [(i, i ^ bit) for i in range(count)]


def on_device(frames, conv_first, second_kernel_weight, conv_third, observe_map, skew_source, retain):
    local, width = retain.shape
    count_x, count_y, count_z = lax.axis_size("x"), lax.axis_size("y"), lax.axis_size("z")
    total_frames = local * count_x * count_y * count_z * lax.axis_size("core")
    me_x = lax.axis_index("x")
    square, vector = (width, width), (8, width)

    keeps = around(retain, "y", count_y)
    factor = float(np.float32(0.7) / np.sqrt(np.float32(total_frames)))
    top, rest = call(functools.partial(turn_kernel, factor), [(square, BF16)] * 2, [], 10**9, 10**6, skew_source)
    drive = encode(frames, conv_first, second_kernel_weight, conv_third, observe_map, retain)
    pushes = around(drive, "y", count_y)

    top, rest, _ = lax.optimization_barrier((top, rest, drive))
    maps, block_map, own_map = call(
        maps_kernel,
        [((count_y,) + square, F32), (square, F32), (square, F32)],
        [((count_y, local, width), F32)],
        4 * 10**9,
        2 * 10**6,
        top,
        rest,
        *keeps,
    )
    block_end, own_entry = call(
        local_kernel,
        [(vector, F32)] * 2,
        [((count_y, local, width), F32)] * 2,
        10**9,
        2 * 10**6,
        top,
        rest,
        maps,
        *keeps,
        *pushes,
    )

    levels = [("z", 1 << k, count_z) for k in range(count_z.bit_length() - 1)] + [("core", 1, 2)]
    for axis, bit, count in levels:
        pairs = exchange_pairs(bit, count)
        upper = (lax.axis_index(axis) & bit) > 0
        other_end = lax.ppermute(block_end[:1], axis, pairs)
        other_map = lax.ppermute(block_map, axis, pairs)
        low = jnp.where(upper, other_map, block_map)
        high = jnp.where(upper, block_map, other_map)
        low_end = jnp.where(upper, other_end, block_end[:1])
        high_end = jnp.where(upper, block_end[:1], other_end)
        own_entry = jnp.where(upper, dot(low_end, own_map) + own_entry, own_entry)
        own_map = jnp.where(upper, dot(low, own_map), own_map)
        block_end = dot(low_end, high) + high_end
        block_map = dot(low, high)

    entry = jnp.zeros((1, width), F32)
    leaving = block_end
    for hop in range(count_x - 1):
        arrived = lax.ppermute(leaving, "x", [(hop, hop + 1)])
        entry = jnp.where(me_x == hop + 1, arrived, entry)
        if hop + 2 < count_x:
            leaving = dot(entry, block_map) + block_end

    (filtered,) = call(
        final_kernel,
        [((local, width), F32)],
        [],
        10**8,
        10**6,
        top,
        rest,
        jnp.broadcast_to(entry, vector),
        own_map,
        own_entry,
        retain,
        drive,
    )
    return filtered


def solution(mesh):
    grp, seg = mesh.shape["grp"], mesh.shape["seg"]
    parts = Mesh(mesh.devices.reshape(grp // 2, 2, seg // 4, 4), ("x", "core", "z", "y"))
    whole = ("x", "core", "z", "y")
    placed = (P(whole), P(), P(), P(), P(), P(), P(whole))
    return jax.shard_map(on_device, mesh=parts, in_specs=placed, out_specs=P(whole), check_vma=False)
```

```python
import functools

import jax
import jax.numpy as jnp
import numpy as np
from jax import lax
from jax.experimental import pallas as pl
from jax.experimental.pallas import tpu as pltpu
from jax.sharding import Mesh, PartitionSpec as P

VMEM = pl.BlockSpec(memory_space=pltpu.VMEM)
LIMIT = 24 * 1024 * 1024
F32, BF16 = jnp.float32, jnp.bfloat16


def halves(value):
    top = value.astype(BF16)
    return top, (value - top.astype(F32)).astype(BF16)


def dot3(left, right):
    (left_top, left_rest), (right_top, right_rest) = left, right
    return (
        jnp.dot(left_top, right_rest, preferred_element_type=F32)
        + jnp.dot(left_rest, right_top, preferred_element_type=F32)
    ) + jnp.dot(left_top, right_top, preferred_element_type=F32)


def product(left, right):
    return dot3(halves(left), halves(right))


def call(kernel, outs, scratch, flops, traffic, *args):
    return pl.pallas_call(
        kernel,
        out_shape=[jax.ShapeDtypeStruct(shape, kind) for shape, kind in outs],
        in_specs=[VMEM] * len(args),
        out_specs=[VMEM] * len(outs),
        scratch_shapes=[pltpu.VMEM(shape, kind) for shape, kind in scratch],
        compiler_params=pltpu.CompilerParams(vmem_limit_bytes=LIMIT),
        cost_estimate=pl.CostEstimate(flops=flops, bytes_accessed=traffic, transcendentals=0),
    )(*args)


def rows_of(store, step, first, length):
    ways = store.shape[0]
    pieces = []
    for turn in range(ways // step):
        row = first + step * turn
        pieces.append(store[row % ways, pl.ds(row // ways, length * step // ways)])
    return pieces


def put_rows(store, value, first, start, size):
    ways = store.shape[0]
    share = value.shape[0] // ways
    for turn in range(ways):
        row = first + turn
        store[row % ways, pl.ds(row // ways, share), :, start : start + size] = value[turn * share : (turn + 1) * share]


def clear_rows(store, rows):
    for row in rows:
        store[row % store.shape[0], row // store.shape[0]] = jnp.zeros(store.shape[2:], F32)


def flatten(pieces, start, size):
    return jnp.concatenate([p[:, :, start : start + size].reshape(-1, size) for p in pieces], 0).astype(BF16)


def turn_of(source, factor):
    width = source.shape[0]
    skew = (source.T - source) * factor
    first = halves(skew)
    two = dot3(first, first)
    square = halves(two)
    three = dot3(first, square)
    four = dot3(square, square)
    row = lax.broadcasted_iota(jnp.int32, (width, width), 0)
    eye = (row == lax.broadcasted_iota(jnp.int32, (width, width), 1)).astype(F32)
    upper = eye / 24.0 + skew / 120.0 + two / 720.0 + three / 5040.0 + four / 40320.0
    return halves(skew + two / 2.0 + three / 6.0 + product(four, upper))


def encoder_kernel(factor, *refs):
    far, (raw, top, rest), near = refs[:7], refs[7:10], refs[10:17]
    flat, lines, wide, one, two, arrived = refs[17:]
    copies = [pltpu.make_async_copy(far[k], near[k], arrived.at[k]) for k in range(7)]
    for copy in copies[:3]:
        copy.start()
    source, frames, kernel, second, third, observe, retain = near
    count, height, row = frames.shape
    lanes = lines.shape[3]
    wide[...] = jnp.zeros_like(wide)
    clear_rows(lines, (0, height + 1))
    clear_rows(one, (0, height // 2 + 1))
    clear_rows(two, (0, height // 4 + 1))
    edge = jnp.zeros(two.shape[:3] + (128,), F32)
    two[:, :, :, :128] = edge
    two[:, :, :, two.shape[3] - 128 :] = edge
    for copy in copies[:3]:
        copy.wait()
    for copy in copies[3:]:
        copy.start()
    top[...], rest[...] = turn_of(source[...], factor)
    pixels = frames[...].astype(F32).reshape(count * height, row)
    pixels = jnp.concatenate([pixels, jnp.zeros((count * height, lanes - row), F32)], 1)
    pixels = pltpu.roll(pixels, 9, 1)
    flat[0] = pixels[:, :128]
    flat[1] = pixels[:, 128:]
    for h in range(height):
        for side in range(2):
            picked = flat[side, pl.ds(h, count, stride=height), :]
            lines[(h + 1) % 8, (h + 1) // 8, :, 128 * side : 128 * side + 128] = picked
    taps, depth, broad = kernel.shape[0], 64, wide.shape[2]
    room = lanes - depth
    for tap in range(taps):
        base = [kernel[tap, k].astype(F32) for k in range(taps)]
        base = jnp.concatenate(base + [jnp.zeros((depth - 12, 64), F32)], 0)
        band = jnp.concatenate([base] + [pltpu.roll(base, 6 * k, 0) for k in range(1, 8)], 1)
        wide[tap, room : room + depth, :] = band.astype(BF16)

    rows = height // 2
    sources = [flatten(rows_of(lines, 2, tap, rows), 0, lanes) for tap in range(taps)]
    halved = [[jnp.concatenate([p[:, k : k + 128] for p in sources[t : t + 2]], 1) for k in (0, 128)] for t in (0, 2)]
    total = one.shape[3]
    for start in range(0, total, broad):
        size = min(broad, total - start)
        shift = start // broad * 48
        value = None
        for side in range(2):
            if shift >= 128 * (side + 1) or shift + 54 <= 128 * side:
                continue
            first = room - shift + 128 * side
            for pair in range(2):
                weights = [wide[2 * pair + k, first : first + 128, :size] for k in range(2)]
                part = jnp.dot(halved[pair][side], jnp.concatenate(weights, 0), preferred_element_type=F32)
                value = part if value is None else value + part
        value = jnp.maximum(value, 0.0).astype(BF16).astype(F32)
        lane = lax.broadcasted_iota(jnp.int32, value.shape, 1) + start
        if start == 0:
            value = jnp.where(lane >= 64, value, 0.0)
        if start + size == total:
            value = jnp.where(lane < total - 64, value, 0.0)
        put_rows(one, value.reshape(rows, count, size), 1, start, size)

    copies[3].wait()
    rows = rows // 2
    weights = []
    for pair in range(2):
        taps_of = [second[2 * pair + k] for k in range(2)]
        sides = [jnp.concatenate([t[128 * side : 128 * side + 128] for t in taps_of], 0) for side in range(2)]
        weights.append(jnp.concatenate(sides, 1))
    left = None
    for tile in range(rows + 1):
        lanes_of = slice(128 * tile, 128 * tile + 128)
        value = None
        for pair in range(2):
            pieces = [flatten([p[:, :, lanes_of] for p in rows_of(one, 2, 2 * pair + k, rows)], 0, 128) for k in range(2)]
            part = jnp.dot(jnp.concatenate(pieces, 1), weights[pair], preferred_element_type=F32)
            value = part if value is None else value + part
        if tile > 0:
            result = jnp.maximum(left + value[:, 128:], 0.0).astype(BF16).astype(F32)
            put_rows(two, result.reshape(rows, count, 128), 1, 128 * tile, 128)
        left = value[:, :128]

    for copy in copies[4:]:
        copy.wait()
    rows = rows // 2
    value = jnp.zeros((rows * rows * count, third.shape[2]), F32)
    for tap in range(4):
        pieces = [flatten(rows_of(two, 2, tap, rows), 256 * j, 512) for j in range(rows)]
        value += jnp.dot(jnp.concatenate(pieces, 0), third[tap], preferred_element_type=F32)
    value = jnp.maximum(value, 0.0).reshape(rows * rows, count, value.shape[1])
    pooled = (jnp.sum(value, 0) * (1.0 / (rows * rows))).astype(BF16)
    raw[:count, :] = retain[...]
    raw[count:, :] = (1.0 - retain[...]) * jnp.dot(pooled, observe[...], preferred_element_type=F32)


def encode(factor, frames, conv_first, second_kernel_weight, conv_third, observe_map, skew_source, retain):
    count, height, row = frames.shape
    local, width = retain.shape
    far = [
        skew_source,
        frames,
        conv_first,
        second_kernel_weight.reshape(4, 256, 128),
        conv_third.reshape(4, 512, 256),
        observe_map,
        retain,
    ]
    outs = [((2 * local, width), F32), ((width, width), BF16), ((width, width), BF16)]
    scratch = [
        ((2, count * height, 128), F32),
        ((8, height // 8 + 1, count, 256), F32),
        ((4, 448, 512), BF16),
        ((4, height // 8 + 1, count, 34 * 64), F32),
        ((2, height // 8 + 1, count, 18 * 128), F32),
    ]
    return pl.pallas_call(
        functools.partial(encoder_kernel, factor),
        out_shape=[jax.ShapeDtypeStruct(shape, kind) for shape, kind in outs],
        in_specs=[pl.BlockSpec(memory_space=pltpu.HBM)] * len(far),
        out_specs=[VMEM] * len(outs),
        scratch_shapes=[pltpu.VMEM(a.shape, a.dtype) for a in far]
        + [pltpu.VMEM(shape, kind) for shape, kind in scratch]
        + [pltpu.SemaphoreType.DMA((len(far),))],
        compiler_params=pltpu.CompilerParams(vmem_limit_bytes=60 * 1024 * 1024),
        cost_estimate=pl.CostEstimate(flops=5 * 10**9, bytes_accessed=2 * 10**6, transcendentals=0),
    )(*far)


def maps_kernel(mine, top, rest, raw, *refs):
    refs, place = refs[:-1], refs[-1]
    groups, count, rows, width = place.shape
    local, spare = rows // 2, 16
    me = lax.axis_index("y")
    for group in range(groups):
        for slot in range(count):
            piece = raw[(group * count + slot) * rows : (group * count + slot + 1) * rows, :]
            place[group, pl.ds(lax.bitwise_xor(me, slot), 1)] = piece[None]
    turn = (top[...], rest[...])
    row = lax.broadcasted_iota(jnp.int32, (width, width), 0)
    eye = (row == lax.broadcasted_iota(jnp.int32, (width, width), 1)).astype(F32)
    start = eye + (turn[0].astype(F32) + turn[1].astype(F32))
    total = groups * count

    def line(block, step):
        return place[block // count, block % count, step : step + 1, :]

    def stack(step):
        lines = [line(block, step) for block in range(total)]
        return jnp.concatenate(lines + [jnp.zeros((spare - total, width), F32)], 0)

    values = [start * line(block, 0) for block in range(total)]
    states = stack(local)
    for step in range(1, local):
        both = jnp.concatenate([values[0], states], 0)
        both = both + dot3(halves(both), turn)
        states = both[width:] * stack(step) + stack(local + step)
        values[0] = both[:width] * line(0, step)
        for block in range(1, total):
            values[block] = (values[block] + dot3(halves(values[block]), turn)) * line(block, step)

    def spread(block):
        return jnp.broadcast_to(states[block : block + 1], (spare, width))

    for group in range(groups):
        before = jnp.concatenate([values[group * count], spread(group * count)], 0)
        prefix = jnp.concatenate([eye, jnp.zeros((spare, width), F32)], 0)
        for k in range(1, count):
            block = group * count + k
            if mine:
                prefix = jnp.where(me == k, before, prefix)
            later = product(before, values[block])
            before = jnp.concatenate([later[:width], later[width:] + spread(block)], 0)
        refs[0][group] = before[: width + 8]
        if mine:
            refs[1][...] = prefix[: width + 8]


def group_maps(mine, top, rest, raw, width):
    rows = raw.shape[0]
    groups = rows // 64
    outs = [((groups, width + 8, width), F32)] + [((width + 8, width), F32)] * mine
    scratch = [((groups, 4, 16, width), F32)]
    cost = 4 * 10**9 * groups
    return call(functools.partial(maps_kernel, mine), outs, scratch, cost, 2 * 10**6, top, rest, raw)


def ahead_kernel(top, rest, own, raw, maps_top, maps_rest, states):
    turn = (top[...], rest[...])
    width, local = own.shape[1], states.shape[0]
    value, state = own[:width, :], own[width:, :]
    for step in range(local):
        keep = raw[step : step + 1, :]
        value = (value + dot3(halves(value), turn)) * keep
        state = (state + dot3(halves(state), turn)) * keep + raw[local + step : local + step + 1, :]
        lanes = slice(step * width, (step + 1) * width)
        maps_top[:, lanes], maps_rest[:, lanes] = halves(value)
        states[step : step + 1, :] = state[0:1]


def final_kernel(entry, late, maps_top, maps_rest, states, out):
    width = states.shape[1]
    state = product(jnp.broadcast_to(entry[...], (8, width)), late[:width, :]) + late[width:, :]
    rows = dot3(halves(state), (maps_top[...], maps_rest[...]))
    for step in range(states.shape[0]):
        out[step : step + 1, :] = rows[0:1, step * width : (step + 1) * width] + states[step : step + 1, :]


def dot(a, b):
    return jnp.dot(a, b, precision=lax.Precision.HIGH, preferred_element_type=F32)


def exchange_pairs(bit, count):
    if 2 * bit == count:
        return [(i, count - 1 - i) for i in range(count)]
    return [(i, i ^ bit) for i in range(count)]


def join(low, high):
    width = low.shape[1]
    return dot(low, high[:width]) + jnp.concatenate([jnp.zeros((width, width), F32), high[width:]], 0)


def on_device(frames, conv_first, second_kernel_weight, conv_third, observe_map, skew_source, retain):
    local, width = retain.shape
    count_x, count_y, count_z = lax.axis_size("x"), lax.axis_size("y"), lax.axis_size("z")
    total_frames = local * count_x * count_y * count_z * lax.axis_size("core")
    me_x, me_z, me_core = lax.axis_index("x"), lax.axis_index("z"), lax.axis_index("core")
    factor = float(np.float32(0.7) / np.sqrt(np.float32(total_frames)))

    raw, top, rest = encode(
        factor, frames, conv_first, second_kernel_weight, conv_third, observe_map, skew_source, retain
    )
    pieces = [lax.ppermute(raw, "y", [(i, i ^ k) for i in range(count_y)]) for k in range(1, count_y)]
    rows = jnp.concatenate([raw] + pieces, 0)
    beside = lax.ppermute(rows, "z", exchange_pairs(1, count_z))
    group, own = group_maps(True, top, rest, rows, width)
    beside, group = lax.optimization_barrier((beside, group))
    across = lax.ppermute(jnp.concatenate([rows, beside], 0), "z", exchange_pairs(2, count_z))
    (other,) = group_maps(False, top, rest, beside, width)
    across, other = lax.optimization_barrier((across, other))
    (others,) = group_maps(False, top, rest, across, width)

    odd, second = (me_z & 1) > 0, (me_z & 2) > 0
    low, high = jnp.where(odd, other[0], group[0]), jnp.where(odd, group[0], other[0])
    own = jnp.where(odd, join(low, own), own)
    pair = join(low, high)
    low, high = jnp.where(odd, others[1], others[0]), jnp.where(odd, others[0], others[1])
    other_pair = join(low, high)
    low, high = jnp.where(second, other_pair, pair), jnp.where(second, pair, other_pair)
    own = jnp.where(second, join(low, own), own)
    block = join(low, high)

    other = lax.ppermute(block, "z", exchange_pairs(4, count_z))
    ahead = call(
        ahead_kernel,
        [((width, local * width), BF16)] * 2 + [((local, width), F32)],
        [],
        10**9,
        10**6,
        top,
        rest,
        own,
        raw,
    )
    other, *ahead = lax.optimization_barrier((other, *ahead))
    upper = (me_z & 4) > 0
    low_half = jnp.where(upper, other, block)
    block = join(low_half, jnp.where(upper, block, other))

    other = lax.ppermute(block, "core", exchange_pairs(1, 2))
    low_core, high_core = jnp.where(me_core > 0, other, block), jnp.where(me_core > 0, block, other)
    block_end = dot(low_core[width : width + 1], high_core[:width]) + high_core[width : width + 1]
    block_end, low_core = lax.optimization_barrier((block_end, low_core))

    first_end = lax.ppermute(block_end, "x", [(0, 1)])
    block = join(low_core, high_core)
    third = lax.ppermute(block, "x", [(2, 3)])
    still = jnp.concatenate([jnp.eye(width, dtype=F32), jnp.zeros((8, width), F32)], 0)
    late = join(jnp.where(me_core > 0, low_core, still), jnp.where(upper, low_half, still))
    leaving = dot(first_end, block[:width]) + block_end
    for_fourth = lax.ppermute(leaving, "x", [(1, 3)])
    for_third = lax.ppermute(leaving, "x", [(1, 2)])
    entry = dot(for_fourth, third[:width]) + third[width : width + 1]
    entry = jnp.where(me_x == 1, first_end, jnp.where(me_x == 2, for_third, entry))

    (filtered,) = call(
        final_kernel, [((local, width), F32)], [], 10**8, 10**6, entry, late, *ahead
    )
    return filtered


def solution(mesh):
    grp, seg = mesh.shape["grp"], mesh.shape["seg"]
    parts = Mesh(mesh.devices.reshape(grp // 2, 2, seg // 4, 4), ("x", "core", "z", "y"))
    whole = ("x", "core", "z", "y")
    placed = (P(whole), P(), P(), P(), P(), P(), P(whole))
    return jax.shard_map(on_device, mesh=parts, in_specs=placed, out_specs=P(whole), check_vma=False)
```

```python
import functools

import jax
import jax.numpy as jnp
import numpy as np
from jax import lax
from jax.experimental import pallas as pl
from jax.experimental.pallas import tpu as pltpu
from jax.sharding import Mesh, PartitionSpec as P

VMEM = pl.BlockSpec(memory_space=pltpu.VMEM)
LIMIT = 24 * 1024 * 1024
F32, BF16 = jnp.float32, jnp.bfloat16


def halves(value):
    top = value.astype(BF16)
    return top, (value - top.astype(F32)).astype(BF16)


def dot3(left, right):
    (left_top, left_rest), (right_top, right_rest) = left, right
    return (
        jnp.dot(left_top, right_rest, preferred_element_type=F32)
        + jnp.dot(left_rest, right_top, preferred_element_type=F32)
    ) + jnp.dot(left_top, right_top, preferred_element_type=F32)


def product(left, right):
    return dot3(halves(left), halves(right))


def call(kernel, outs, scratch, flops, traffic, *args):
    return pl.pallas_call(
        kernel,
        out_shape=[jax.ShapeDtypeStruct(shape, kind) for shape, kind in outs],
        in_specs=[VMEM] * len(args),
        out_specs=[VMEM] * len(outs),
        scratch_shapes=[pltpu.VMEM(shape, kind) for shape, kind in scratch],
        compiler_params=pltpu.CompilerParams(vmem_limit_bytes=LIMIT),
        cost_estimate=pl.CostEstimate(flops=flops, bytes_accessed=traffic, transcendentals=0),
    )(*args)


def rows_of(store, step, first, length):
    ways = store.shape[0]
    pieces = []
    for turn in range(ways // step):
        row = first + step * turn
        pieces.append(store[row % ways, pl.ds(row // ways, length * step // ways)])
    return pieces


def put_rows(store, value, first, start, size):
    ways = store.shape[0]
    share = value.shape[0] // ways
    for turn in range(ways):
        row = first + turn
        store[row % ways, pl.ds(row // ways, share), :, start : start + size] = value[turn * share : (turn + 1) * share]


def clear_rows(store, rows):
    for row in rows:
        store[row % store.shape[0], row // store.shape[0]] = jnp.zeros(store.shape[2:], F32)


def flatten(pieces, start, size):
    return jnp.concatenate([p[:, :, start : start + size].reshape(-1, size) for p in pieces], 0).astype(BF16)


def turn_kernel(factor, source, top, rest):
    width = source.shape[0]
    skew = (source[...].T - source[...]) * factor
    first = halves(skew)
    two = dot3(first, first)
    square = halves(two)
    three = dot3(first, square)
    four = dot3(square, square)
    row = lax.broadcasted_iota(jnp.int32, (width, width), 0)
    eye = (row == lax.broadcasted_iota(jnp.int32, (width, width), 1)).astype(F32)
    upper = eye / 24.0 + skew / 120.0 + two / 720.0 + three / 5040.0 + four / 40320.0
    top[...], rest[...] = halves(skew + two / 2.0 + three / 6.0 + product(four, upper))


def encoder_kernel(*refs):
    far, raw, near = refs[:6], refs[6], refs[7:13]
    flat, lines, wide, one, two, arrived = refs[13:]
    copies = [pltpu.make_async_copy(far[k], near[k], arrived.at[k]) for k in range(6)]
    for copy in copies[:2]:
        copy.start()
    frames, kernel, second, third, observe, retain = near
    count, height, row = frames.shape
    lanes = lines.shape[3]
    wide[...] = jnp.zeros_like(wide)
    clear_rows(lines, (0, height + 1))
    clear_rows(one, (0, height // 2 + 1))
    clear_rows(two, (0, height // 4 + 1))
    edge = jnp.zeros(two.shape[:3] + (128,), F32)
    two[:, :, :, :128] = edge
    two[:, :, :, two.shape[3] - 128 :] = edge
    for copy in copies[:2]:
        copy.wait()
    for copy in copies[2:]:
        copy.start()
    pixels = frames[...].astype(F32).reshape(count * height, row)
    pixels = jnp.concatenate([pixels, jnp.zeros((count * height, lanes - row), F32)], 1)
    pixels = pltpu.roll(pixels, 9, 1)
    flat[0] = pixels[:, :128]
    flat[1] = pixels[:, 128:]
    for h in range(height):
        for side in range(2):
            picked = flat[side, pl.ds(h, count, stride=height), :]
            lines[(h + 1) % 8, (h + 1) // 8, :, 128 * side : 128 * side + 128] = picked
    taps, depth, broad = kernel.shape[0], 64, wide.shape[2]
    room = lanes - depth
    for tap in range(taps):
        colours = [kernel[tap, c].astype(F32) for c in range(3)]
        base = [colours[c][k : k + 1] for k in range(taps) for c in range(3)]
        base = jnp.concatenate(base + [jnp.zeros((depth - 12, 64), F32)], 0)
        band = jnp.concatenate([base] + [pltpu.roll(base, 6 * k, 0) for k in range(1, 8)], 1)
        wide[tap, room : room + depth, :] = band.astype(BF16)

    rows = height // 2
    sources = [flatten(rows_of(lines, 2, tap, rows), 0, lanes) for tap in range(taps)]
    halved = [[jnp.concatenate([p[:, k : k + 128] for p in sources[t : t + 2]], 1) for k in (0, 128)] for t in (0, 2)]
    total = one.shape[3]
    for start in range(0, total, broad):
        size = min(broad, total - start)
        shift = start // broad * 48
        value = None
        for side in range(2):
            if shift >= 128 * (side + 1) or shift + 54 <= 128 * side:
                continue
            first = room - shift + 128 * side
            for pair in range(2):
                weights = [wide[2 * pair + k, first : first + 128, :size] for k in range(2)]
                part = jnp.dot(halved[pair][side], jnp.concatenate(weights, 0), preferred_element_type=F32)
                value = part if value is None else value + part
        value = jnp.maximum(value, 0.0).astype(BF16).astype(F32)
        lane = lax.broadcasted_iota(jnp.int32, value.shape, 1) + start
        if start == 0:
            value = jnp.where(lane >= 64, value, 0.0)
        if start + size == total:
            value = jnp.where(lane < total - 64, value, 0.0)
        put_rows(one, value.reshape(rows, count, size), 1, start, size)

    copies[2].wait()
    rows = rows // 2
    weights = []
    for pair in range(2):
        taps_of = [second[2 * pair + k] for k in range(2)]
        sides = [jnp.concatenate([t[128 * side : 128 * side + 128] for t in taps_of], 0) for side in range(2)]
        weights.append(jnp.concatenate(sides, 1))
    left = None
    for tile in range(rows + 1):
        lanes_of = slice(128 * tile, 128 * tile + 128)
        value = None
        for pair in range(2):
            pieces = [flatten([p[:, :, lanes_of] for p in rows_of(one, 2, 2 * pair + k, rows)], 0, 128) for k in range(2)]
            part = jnp.dot(jnp.concatenate(pieces, 1), weights[pair], preferred_element_type=F32)
            value = part if value is None else value + part
        if tile > 0:
            result = jnp.maximum(left + value[:, 128:], 0.0).astype(BF16).astype(F32)
            put_rows(two, result.reshape(rows, count, 128), 1, 128 * tile, 128)
        left = value[:, :128]

    for copy in copies[3:]:
        copy.wait()
    rows = rows // 2
    value = jnp.zeros((rows * rows * count, third.shape[2]), F32)
    for tap in range(4):
        pieces = [flatten(rows_of(two, 2, tap, rows), 256 * j, 512) for j in range(rows)]
        value += jnp.dot(jnp.concatenate(pieces, 0), third[tap], preferred_element_type=F32)
    value = jnp.maximum(value, 0.0).reshape(rows * rows, count, value.shape[1])
    pooled = (jnp.sum(value, 0) * (1.0 / (rows * rows))).astype(BF16)
    raw[:count, :] = retain[...]
    raw[count:, :] = (1.0 - retain[...]) * jnp.dot(pooled, observe[...], preferred_element_type=F32)


def encode(frames, conv_first, second_kernel_weight, conv_third, observe_map, retain):
    count, height, row = frames.shape
    local, width = retain.shape
    far = [
        frames,
        jnp.transpose(conv_first, (0, 2, 1, 3)),
        second_kernel_weight.reshape(4, 256, 128),
        conv_third.reshape(4, 512, 256),
        observe_map,
        retain,
    ]
    scratch = [
        ((2, count * height, 128), F32),
        ((8, height // 8 + 1, count, 256), F32),
        ((4, 448, 512), BF16),
        ((4, height // 8 + 1, count, 34 * 64), F32),
        ((2, height // 8 + 1, count, 18 * 128), F32),
    ]
    return pl.pallas_call(
        encoder_kernel,
        out_shape=jax.ShapeDtypeStruct((2 * local, width), F32),
        in_specs=[pl.BlockSpec(memory_space=pltpu.HBM)] * len(far),
        out_specs=VMEM,
        scratch_shapes=[pltpu.VMEM(a.shape, a.dtype) for a in far]
        + [pltpu.VMEM(shape, kind) for shape, kind in scratch]
        + [pltpu.SemaphoreType.DMA((len(far),))],
        compiler_params=pltpu.CompilerParams(vmem_limit_bytes=60 * 1024 * 1024),
        cost_estimate=pl.CostEstimate(flops=5 * 10**9, bytes_accessed=2 * 10**6, transcendentals=0),
    )(*far)


def maps_kernel(mine, top, rest, raw, *refs):
    refs, place = refs[:-1], refs[-1]
    groups, count, rows, width = place.shape
    known = refs[0] if groups == 2 else None
    refs = refs[1:] if groups == 2 else refs
    local, spare = rows // 2, 16
    me = lax.axis_index("y")
    for group in range(groups):
        for slot in range(count):
            piece = raw[(group * count + slot) * rows : (group * count + slot + 1) * rows, :]
            place[group, pl.ds(lax.bitwise_xor(me, slot), 1)] = piece[None]
    turn = (top[...], rest[...])
    row = lax.broadcasted_iota(jnp.int32, (width, width), 0)
    eye = (row == lax.broadcasted_iota(jnp.int32, (width, width), 1)).astype(F32)
    start = eye + (turn[0].astype(F32) + turn[1].astype(F32))
    total = groups * count

    def line(block, step):
        return place[block // count, block % count, step : step + 1, :]

    def stack(step):
        lines = [line(block, step) for block in range(total)]
        return jnp.concatenate(lines + [jnp.zeros((spare - total, width), F32)], 0)

    values = [start * line(block, 0) for block in range(total)]
    states = stack(local)
    for step in range(1, local):
        both = jnp.concatenate([values[0], states], 0)
        both = both + dot3(halves(both), turn)
        states = both[width:] * stack(step) + stack(local + step)
        values[0] = both[:width] * line(0, step)
        for block in range(1, total):
            values[block] = (values[block] + dot3(halves(values[block]), turn)) * line(block, step)

    def spread(block):
        return jnp.broadcast_to(states[block : block + 1], (spare, width))

    results = []
    for group in range(groups):
        before = jnp.concatenate([values[group * count], spread(group * count)], 0)
        prefix = jnp.concatenate([eye, jnp.zeros((spare, width), F32)], 0)
        for k in range(1, count):
            block = group * count + k
            if mine:
                prefix = jnp.where(me == k, before, prefix)
            later = product(before, values[block])
            before = jnp.concatenate([later[:width], later[width:] + spread(block)], 0)
        results.append(before)
        if mine:
            refs[1][...] = prefix[: width + 8]
    if groups == 1:
        refs[0][...] = results[0][: width + 8]
        return

    def joined(first, later):
        result = product(first, later[:width])
        return jnp.concatenate([result[:width], result[width:] + later[width:]], 0)

    z = lax.axis_index("z")
    odd, second = lax.rem(z, 2) == 1, lax.rem(z, 4) >= 2
    pair = joined(*(jnp.where(odd, results[1 - k], results[k]) for k in range(2)))
    known = jnp.concatenate([known[...], known[width:, :]], 0)
    refs[0][...] = joined(jnp.where(second, pair, known), jnp.where(second, known, pair))[: width + 8]
    refs[1][...] = pair[: width + 8]


def group_maps(mine, top, rest, raw, *known):
    width, groups = raw.shape[1], raw.shape[0] // 64
    outs = [((width + 8, width), F32)] * (2 if mine or known else 1)
    scratch = [((groups, 4, 16, width), F32)]
    cost = 4 * 10**9 * groups
    return call(functools.partial(maps_kernel, mine), outs, scratch, cost, 2 * 10**6, top, rest, raw, *known)


def ahead_kernel(top, rest, own, raw, maps_top, maps_rest, states):
    turn = (top[...], rest[...])
    width, local = own.shape[1], states.shape[0]
    value, state = own[:width, :], own[width:, :]
    for step in range(local):
        keep = raw[step : step + 1, :]
        value = (value + dot3(halves(value), turn)) * keep
        state = (state + dot3(halves(state), turn)) * keep + raw[local + step : local + step + 1, :]
        lanes = slice(step * width, (step + 1) * width)
        maps_top[:, lanes], maps_rest[:, lanes] = halves(value)
        states[step : step + 1, :] = state[0:1]


def final_kernel(entry, late, maps_top, maps_rest, states, out):
    width = states.shape[1]
    state = product(jnp.broadcast_to(entry[...], (8, width)), late[:width, :]) + late[width:, :]
    rows = dot3(halves(state), (maps_top[...], maps_rest[...]))
    for step in range(states.shape[0]):
        out[step : step + 1, :] = rows[0:1, step * width : (step + 1) * width] + states[step : step + 1, :]


def dot(a, b):
    return jnp.dot(a, b, precision=lax.Precision.HIGH, preferred_element_type=F32)


def exchange_pairs(bit, count):
    if 2 * bit == count:
        return [(i, count - 1 - i) for i in range(count)]
    return [(i, i ^ bit) for i in range(count)]


def join(low, high):
    width = low.shape[1]
    return dot(low, high[:width]) + jnp.concatenate([jnp.zeros((width, width), F32), high[width:]], 0)


def on_device(frames, conv_first, second_kernel_weight, conv_third, observe_map, skew_source, retain):
    local, width = retain.shape
    count_x, count_y, count_z = lax.axis_size("x"), lax.axis_size("y"), lax.axis_size("z")
    total_frames = local * count_x * count_y * count_z * lax.axis_size("core")
    me_x, me_z, me_core = lax.axis_index("x"), lax.axis_index("z"), lax.axis_index("core")
    factor = float(np.float32(0.7) / np.sqrt(np.float32(total_frames)))

    raw = encode(frames, conv_first, second_kernel_weight, conv_third, observe_map, retain)
    skew_source, raw = lax.optimization_barrier((skew_source, raw))
    square = ((width, width), BF16)
    top, rest = call(functools.partial(turn_kernel, factor), [square] * 2, [], 10**9, 10**6, skew_source)
    pieces = [lax.ppermute(raw, "y", [(i, i ^ k) for i in range(count_y)]) for k in range(1, count_y)]
    rows = jnp.concatenate([raw] + pieces, 0)
    beside = lax.ppermute(rows, "z", exchange_pairs(1, count_z))
    group, own = group_maps(True, top, rest, rows)
    beside, group = lax.optimization_barrier((beside, group))
    across = lax.ppermute(jnp.concatenate([rows, beside], 0), "z", exchange_pairs(2, count_z))
    (other,) = group_maps(False, top, rest, beside)
    across, other = lax.optimization_barrier((across, other))

    odd, second = (me_z & 1) > 0, (me_z & 2) > 0
    low, high = jnp.where(odd, other, group), jnp.where(odd, group, other)
    pair = join(low, high)
    block, other_pair = group_maps(False, top, rest, across, pair)
    own = jnp.where(odd, join(low, own), own)

    other = lax.ppermute(block, "z", exchange_pairs(4, count_z))
    own = jnp.where(second, join(other_pair, own), own)
    ahead = call(
        ahead_kernel,
        [((width, local * width), BF16)] * 2 + [((local, width), F32)],
        [],
        10**9,
        10**6,
        top,
        rest,
        own,
        raw,
    )
    other, *ahead = lax.optimization_barrier((other, *ahead))
    upper = (me_z & 4) > 0
    low_half = jnp.where(upper, other, block)
    block = join(low_half, jnp.where(upper, block, other))

    other = lax.ppermute(block, "core", exchange_pairs(1, 2))
    low_core, high_core = jnp.where(me_core > 0, other, block), jnp.where(me_core > 0, block, other)
    block_end = dot(low_core[width : width + 1], high_core[:width]) + high_core[width : width + 1]
    block_end, low_core = lax.optimization_barrier((block_end, low_core))

    first_end = lax.ppermute(block_end, "x", [(0, 1)])
    block = join(low_core, high_core)
    third = lax.ppermute(block, "x", [(2, 3)])
    still = jnp.concatenate([jnp.eye(width, dtype=F32), jnp.zeros((8, width), F32)], 0)
    late = join(jnp.where(me_core > 0, low_core, still), jnp.where(upper, low_half, still))
    first_end, late = lax.optimization_barrier((first_end, late))
    leaving = dot(first_end, block[:width]) + block_end
    for_fourth = lax.ppermute(leaving, "x", [(1, 3)])
    for_third = lax.ppermute(leaving, "x", [(1, 2)])
    entry = dot(for_fourth, third[:width]) + third[width : width + 1]
    for_third, entry = lax.optimization_barrier((for_third, entry))
    entry = jnp.where(me_x == 1, first_end, jnp.where(me_x == 2, for_third, entry))

    (filtered,) = call(
        final_kernel, [((local, width), F32)], [], 10**8, 10**6, entry, late, *ahead
    )
    return filtered


def solution(mesh):
    grp, seg = mesh.shape["grp"], mesh.shape["seg"]
    parts = Mesh(mesh.devices.reshape(grp // 2, 2, seg // 4, 4), ("x", "core", "z", "y"))
    whole = ("x", "core", "z", "y")
    placed = (P(whole), P(), P(), P(), P(), P(), P(whole))
    return jax.shard_map(on_device, mesh=parts, in_specs=placed, out_specs=P(whole), check_vma=False)
```

```python
import functools

import jax
import jax.numpy as jnp
import numpy as np
from jax import lax
from jax.experimental import pallas as pl
from jax.experimental.pallas import tpu as pltpu
from jax.sharding import Mesh, PartitionSpec as P

VMEM = pl.BlockSpec(memory_space=pltpu.VMEM)
LIMIT = 24 * 1024 * 1024
F32, BF16 = jnp.float32, jnp.bfloat16


def halves(value):
    top = value.astype(BF16)
    return top, (value - top.astype(F32)).astype(BF16)


def dot3(left, right):
    (left_top, left_rest), (right_top, right_rest) = left, right
    return (
        jnp.dot(left_top, right_rest, preferred_element_type=F32)
        + jnp.dot(left_rest, right_top, preferred_element_type=F32)
    ) + jnp.dot(left_top, right_top, preferred_element_type=F32)


def product(left, right):
    return dot3(halves(left), halves(right))


def call(kernel, outs, scratch, flops, traffic, *args):
    return pl.pallas_call(
        kernel,
        out_shape=[jax.ShapeDtypeStruct(shape, kind) for shape, kind in outs],
        in_specs=[VMEM] * len(args),
        out_specs=[VMEM] * len(outs),
        scratch_shapes=[pltpu.VMEM(shape, kind) for shape, kind in scratch],
        compiler_params=pltpu.CompilerParams(vmem_limit_bytes=LIMIT),
        cost_estimate=pl.CostEstimate(flops=flops, bytes_accessed=traffic, transcendentals=0),
    )(*args)


def rows_of(store, step, first, length):
    ways = store.shape[0]
    pieces = []
    for turn in range(ways // step):
        row = first + step * turn
        pieces.append(store[row % ways, pl.ds(row // ways, length * step // ways)])
    return pieces


def put_rows(store, value, first, start, size):
    ways = store.shape[0]
    share = value.shape[0] // ways
    for turn in range(ways):
        row = first + turn
        store[row % ways, pl.ds(row // ways, share), :, start : start + size] = value[turn * share : (turn + 1) * share]


def clear_rows(store, rows):
    for row in rows:
        store[row % store.shape[0], row // store.shape[0]] = jnp.zeros(store.shape[2:], F32)


def flatten(pieces, start, size):
    return jnp.concatenate([p[:, :, start : start + size].reshape(-1, size) for p in pieces], 0).astype(BF16)


def turn_kernel(factor, source, top, rest):
    width = source.shape[0]
    skew = (source[...].T - source[...]) * factor
    first = halves(skew)
    two = dot3(first, first)
    square = halves(two)
    three = dot3(first, square)
    four = dot3(square, square)
    row = lax.broadcasted_iota(jnp.int32, (width, width), 0)
    eye = (row == lax.broadcasted_iota(jnp.int32, (width, width), 1)).astype(F32)
    upper = eye / 24.0 + skew / 120.0 + two / 720.0 + three / 5040.0 + four / 40320.0
    top[...], rest[...] = halves(skew + two / 2.0 + three / 6.0 + product(four, upper))


def encoder_kernel(*refs):
    far, raw, near = refs[:6], refs[6], refs[7:13]
    flat, lines, wide, one, two, arrived = refs[13:]
    copies = [pltpu.make_async_copy(far[k], near[k], arrived.at[k]) for k in range(6)]
    for copy in copies[:2]:
        copy.start()
    frames, kernel, second, third, observe, retain = near
    count, height, row = frames.shape
    lanes = lines.shape[3]
    wide[...] = jnp.zeros_like(wide)
    clear_rows(lines, (0, height + 1))
    clear_rows(one, (0, height // 2 + 1))
    clear_rows(two, (0, height // 4 + 1))
    edge = jnp.zeros(two.shape[:3] + (128,), F32)
    two[:, :, :, :128] = edge
    two[:, :, :, two.shape[3] - 128 :] = edge
    for copy in copies[:2]:
        copy.wait()
    for copy in copies[2:]:
        copy.start()
    pixels = frames[...].astype(F32).reshape(count * height, row)
    pixels = jnp.concatenate([pixels, jnp.zeros((count * height, lanes - row), F32)], 1)
    pixels = pltpu.roll(pixels, 9, 1)
    flat[0] = pixels[:, :128]
    flat[1] = pixels[:, 128:]
    for h in range(height):
        for side in range(2):
            picked = flat[side, pl.ds(h, count, stride=height), :]
            lines[(h + 1) % 8, (h + 1) // 8, :, 128 * side : 128 * side + 128] = picked
    taps, depth, broad = kernel.shape[0], 64, wide.shape[2]
    room = lanes - depth
    for tap in range(taps):
        colours = [kernel[tap, c].astype(F32) for c in range(3)]
        base = [colours[c][k : k + 1] for k in range(taps) for c in range(3)]
        base = jnp.concatenate(base + [jnp.zeros((depth - 12, 64), F32)], 0)
        band = jnp.concatenate([base] + [pltpu.roll(base, 6 * k, 0) for k in range(1, 8)], 1)
        wide[tap, room : room + depth, :] = band.astype(BF16)

    rows = height // 2
    sources = [flatten(rows_of(lines, 2, tap, rows), 0, lanes) for tap in range(taps)]
    halved = [[jnp.concatenate([p[:, k : k + 128] for p in sources[t : t + 2]], 1) for k in (0, 128)] for t in (0, 2)]
    total = one.shape[3]
    for start in range(0, total, broad):
        size = min(broad, total - start)
        shift = start // broad * 48
        value = None
        for side in range(2):
            if shift >= 128 * (side + 1) or shift + 54 <= 128 * side:
                continue
            first = room - shift + 128 * side
            for pair in range(2):
                weights = [wide[2 * pair + k, first : first + 128, :size] for k in range(2)]
                part = jnp.dot(halved[pair][side], jnp.concatenate(weights, 0), preferred_element_type=F32)
                value = part if value is None else value + part
        value = jnp.maximum(value, 0.0).astype(BF16).astype(F32)
        lane = lax.broadcasted_iota(jnp.int32, value.shape, 1) + start
        if start == 0:
            value = jnp.where(lane >= 64, value, 0.0)
        if start + size == total:
            value = jnp.where(lane < total - 64, value, 0.0)
        put_rows(one, value.reshape(rows, count, size), 1, start, size)

    copies[2].wait()
    rows = rows // 2
    weights = []
    for pair in range(2):
        taps_of = [second[2 * pair + k] for k in range(2)]
        sides = [jnp.concatenate([t[128 * side : 128 * side + 128] for t in taps_of], 0) for side in range(2)]
        weights.append(jnp.concatenate(sides, 1))
    left = None
    for tile in range(rows + 1):
        lanes_of = slice(128 * tile, 128 * tile + 128)
        value = None
        for pair in range(2):
            pieces = [flatten([p[:, :, lanes_of] for p in rows_of(one, 2, 2 * pair + k, rows)], 0, 128) for k in range(2)]
            part = jnp.dot(jnp.concatenate(pieces, 1), weights[pair], preferred_element_type=F32)
            value = part if value is None else value + part
        if tile > 0:
            result = jnp.maximum(left + value[:, 128:], 0.0).astype(BF16).astype(F32)
            put_rows(two, result.reshape(rows, count, 128), 1, 128 * tile, 128)
        left = value[:, :128]

    for copy in copies[3:]:
        copy.wait()
    rows = rows // 2
    value = jnp.zeros((rows * rows * count, third.shape[2]), F32)
    for tap in range(4):
        pieces = [flatten(rows_of(two, 2, tap, rows), 256 * j, 512) for j in range(rows)]
        value += jnp.dot(jnp.concatenate(pieces, 0), third[tap], preferred_element_type=F32)
    value = jnp.maximum(value, 0.0).reshape(rows * rows, count, value.shape[1])
    pooled = (jnp.sum(value, 0) * (1.0 / (rows * rows))).astype(BF16)
    raw[:count, :] = retain[...]
    raw[count:, :] = (1.0 - retain[...]) * jnp.dot(pooled, observe[...], preferred_element_type=F32)


def encode(frames, conv_first, second_kernel_weight, conv_third, observe_map, retain):
    count, height, row = frames.shape
    local, width = retain.shape
    far = [
        frames,
        jnp.transpose(conv_first, (0, 2, 1, 3)),
        second_kernel_weight.reshape(4, 256, 128),
        conv_third.reshape(4, 512, 256),
        observe_map,
        retain,
    ]
    scratch = [
        ((2, count * height, 128), F32),
        ((8, height // 8 + 1, count, 256), F32),
        ((4, 448, 512), BF16),
        ((4, height // 8 + 1, count, 34 * 64), F32),
        ((2, height // 8 + 1, count, 18 * 128), F32),
    ]
    return pl.pallas_call(
        encoder_kernel,
        out_shape=jax.ShapeDtypeStruct((2 * local, width), F32),
        in_specs=[pl.BlockSpec(memory_space=pltpu.HBM)] * len(far),
        out_specs=VMEM,
        scratch_shapes=[pltpu.VMEM(a.shape, a.dtype) for a in far]
        + [pltpu.VMEM(shape, kind) for shape, kind in scratch]
        + [pltpu.SemaphoreType.DMA((len(far),))],
        compiler_params=pltpu.CompilerParams(vmem_limit_bytes=60 * 1024 * 1024),
        cost_estimate=pl.CostEstimate(flops=5 * 10**9, bytes_accessed=2 * 10**6, transcendentals=0),
    )(*far)


def maps_kernel(mine, top, rest, raw, *refs):
    refs, place = refs[:-1], refs[-1]
    groups, count, rows, width = place.shape
    known, refs = (refs[:0], refs) if mine else (refs[: 3 - groups], refs[3 - groups :])
    local, spare = rows // 2, 16
    me = lax.axis_index("y")
    for group in range(groups):
        for slot in range(count):
            piece = raw[(group * count + slot) * rows : (group * count + slot + 1) * rows, :]
            place[group, pl.ds(lax.bitwise_xor(me, slot), 1)] = piece[None]
    turn = (top[...], rest[...])
    row = lax.broadcasted_iota(jnp.int32, (width, width), 0)
    eye = (row == lax.broadcasted_iota(jnp.int32, (width, width), 1)).astype(F32)
    start = eye + (turn[0].astype(F32) + turn[1].astype(F32))
    total = groups * count

    def line(block, step):
        return place[block // count, block % count, step : step + 1, :]

    def stack(step):
        lines = [line(block, step) for block in range(total)]
        return jnp.concatenate(lines + [jnp.zeros((spare - total, width), F32)], 0)

    values = [start * line(block, 0) for block in range(total)]
    states = stack(local)
    for step in range(1, local):
        both = jnp.concatenate([values[0], states], 0)
        both = both + dot3(halves(both), turn)
        states = both[width:] * stack(step) + stack(local + step)
        values[0] = both[:width] * line(0, step)
        for block in range(1, total):
            values[block] = (values[block] + dot3(halves(values[block]), turn)) * line(block, step)

    def spread(block):
        return jnp.broadcast_to(states[block : block + 1], (spare, width))

    results = []
    for group in range(groups):
        before = jnp.concatenate([values[group * count], spread(group * count)], 0)
        prefix = jnp.concatenate([eye, jnp.zeros((spare, width), F32)], 0)
        for k in range(1, count):
            block = group * count + k
            if mine:
                prefix = jnp.where(me == k, before, prefix)
            later = product(before, values[block])
            before = jnp.concatenate([later[:width], later[width:] + spread(block)], 0)
        results.append(before)
        if mine:
            refs[1][...] = prefix[: width + 8]
    if mine:
        refs[0][...] = results[0][: width + 8]
        return

    def joined(first, later):
        result = product(first, later[:width])
        return jnp.concatenate([result[:width], result[width:] + later[width:]], 0)

    z = lax.axis_index("z")
    odd, second = lax.rem(z, 2) == 1, lax.rem(z, 4) >= 2
    known = [jnp.concatenate([ref[...], ref[width:, :]], 0) for ref in known]
    if groups == 1:
        group, before = known
        other = results[0]
        refs[0][...] = joined(jnp.where(odd, other, group), jnp.where(odd, group, other))[: width + 8]
        refs[1][...] = jnp.where(odd, joined(other, before), before)[: width + 8]
        return
    pair = joined(*(jnp.where(odd, results[1 - k], results[k]) for k in range(2)))
    refs[0][...] = joined(jnp.where(second, pair, known[0]), jnp.where(second, known[0], pair))[: width + 8]
    refs[1][...] = pair[: width + 8]


def group_maps(mine, top, rest, raw, *known):
    width, groups = raw.shape[1], raw.shape[0] // 64
    outs = [((width + 8, width), F32)] * 2
    scratch = [((groups, 4, 16, width), F32)]
    cost = 4 * 10**9 * groups
    return call(functools.partial(maps_kernel, mine), outs, scratch, cost, 2 * 10**6, top, rest, raw, *known)


def ahead_kernel(top, rest, own, raw, maps_top, maps_rest, states):
    turn = (top[...], rest[...])
    width, local = own.shape[1], states.shape[0]
    value, state = own[:width, :], own[width:, :]
    for step in range(local):
        keep = raw[step : step + 1, :]
        value = (value + dot3(halves(value), turn)) * keep
        state = (state + dot3(halves(state), turn)) * keep + raw[local + step : local + step + 1, :]
        lanes = slice(step * width, (step + 1) * width)
        maps_top[:, lanes], maps_rest[:, lanes] = halves(value)
        states[step : step + 1, :] = state[0:1]


def final_kernel(entry, late, maps_top, maps_rest, states, out):
    width = states.shape[1]
    state = product(jnp.broadcast_to(entry[...], (8, width)), late[:width, :]) + late[width:, :]
    rows = dot3(halves(state), (maps_top[...], maps_rest[...]))
    for step in range(states.shape[0]):
        out[step : step + 1, :] = rows[0:1, step * width : (step + 1) * width] + states[step : step + 1, :]


def dot(a, b):
    return jnp.dot(a, b, precision=lax.Precision.HIGH, preferred_element_type=F32)


def exchange_pairs(bit, count):
    if 2 * bit == count:
        return [(i, count - 1 - i) for i in range(count)]
    return [(i, i ^ bit) for i in range(count)]


def join(low, high):
    width = low.shape[1]
    return dot(low, high[:width]) + jnp.concatenate([jnp.zeros((width, width), F32), high[width:]], 0)


def on_device(frames, conv_first, second_kernel_weight, conv_third, observe_map, skew_source, retain):
    local, width = retain.shape
    count_x, count_y, count_z = lax.axis_size("x"), lax.axis_size("y"), lax.axis_size("z")
    total_frames = local * count_x * count_y * count_z * lax.axis_size("core")
    me_x, me_z, me_core = lax.axis_index("x"), lax.axis_index("z"), lax.axis_index("core")
    factor = float(np.float32(0.7) / np.sqrt(np.float32(total_frames)))

    raw = encode(frames, conv_first, second_kernel_weight, conv_third, observe_map, retain)
    skew_source, raw = lax.optimization_barrier((skew_source, raw))
    square = ((width, width), BF16)
    top, rest = call(functools.partial(turn_kernel, factor), [square] * 2, [], 10**9, 10**6, skew_source)
    pieces = [lax.ppermute(raw, "y", [(i, i ^ k) for i in range(count_y)]) for k in range(1, count_y)]
    rows = jnp.concatenate([raw] + pieces, 0)
    beside = lax.ppermute(rows, "z", exchange_pairs(1, count_z))
    group, own = group_maps(True, top, rest, rows)
    beside, group = lax.optimization_barrier((beside, group))
    across = lax.ppermute(jnp.concatenate([rows, beside], 0), "z", exchange_pairs(2, count_z))
    pair, own = group_maps(False, top, rest, beside, group, own)
    across, pair = lax.optimization_barrier((across, pair))
    block, other_pair = group_maps(False, top, rest, across, pair)
    second = (me_z & 2) > 0

    other = lax.ppermute(block, "z", [(i, i ^ 6) for i in range(count_z)])
    own = jnp.where(second, join(other_pair, own), own)
    ahead = call(
        ahead_kernel,
        [((width, local * width), BF16)] * 2 + [((local, width), F32)],
        [],
        10**9,
        10**6,
        top,
        rest,
        own,
        raw,
    )
    other, *ahead = lax.optimization_barrier((other, *ahead))
    upper = (me_z & 4) > 0
    low_half = jnp.where(upper, other, block)
    block = join(low_half, jnp.where(upper, block, other))

    other = lax.ppermute(block, "core", exchange_pairs(1, 2))
    low_core, high_core = jnp.where(me_core > 0, other, block), jnp.where(me_core > 0, block, other)
    block_end = dot(low_core[width : width + 1], high_core[:width]) + high_core[width : width + 1]
    block_end, low_core = lax.optimization_barrier((block_end, low_core))

    first_end = lax.ppermute(block_end, "x", [(0, 1)])
    block = join(low_core, high_core)
    third = lax.ppermute(block, "x", [(2, 3)])
    still = jnp.concatenate([jnp.eye(width, dtype=F32), jnp.zeros((8, width), F32)], 0)
    late = join(jnp.where(me_core > 0, low_core, still), jnp.where(upper, low_half, still))
    first_end, late = lax.optimization_barrier((first_end, late))
    leaving = dot(first_end, block[:width]) + block_end
    for_fourth = lax.ppermute(leaving, "x", [(1, 3)])
    for_third = lax.ppermute(leaving, "x", [(1, 2)])
    entry = dot(for_fourth, third[:width]) + third[width : width + 1]
    for_third, entry = lax.optimization_barrier((for_third, entry))
    entry = jnp.where(me_x == 1, first_end, jnp.where(me_x == 2, for_third, entry))

    (filtered,) = call(
        final_kernel, [((local, width), F32)], [], 10**8, 10**6, entry, late, *ahead
    )
    return filtered


def solution(mesh):
    grp, seg = mesh.shape["grp"], mesh.shape["seg"]
    parts = Mesh(mesh.devices.reshape(grp // 2, 2, seg // 4, 4), ("x", "core", "z", "y"))
    whole = ("x", "core", "z", "y")
    placed = (P(whole), P(), P(), P(), P(), P(), P(whole))
    return jax.shard_map(on_device, mesh=parts, in_specs=placed, out_specs=P(whole), check_vma=False)
```

```python
import functools

import jax
import jax.numpy as jnp
import numpy as np
from jax import lax
from jax.experimental import pallas as pl
from jax.experimental.pallas import tpu as pltpu
from jax.sharding import Mesh, PartitionSpec as P

VMEM = pl.BlockSpec(memory_space=pltpu.VMEM)
LIMIT = 24 * 1024 * 1024
F32, BF16 = jnp.float32, jnp.bfloat16


def halves(value):
    top = value.astype(BF16)
    return top, (value - top.astype(F32)).astype(BF16)


def dot3(left, right):
    (left_top, left_rest), (right_top, right_rest) = left, right
    return (
        jnp.dot(left_top, right_rest, preferred_element_type=F32)
        + jnp.dot(left_rest, right_top, preferred_element_type=F32)
    ) + jnp.dot(left_top, right_top, preferred_element_type=F32)


def product(left, right):
    return dot3(halves(left), halves(right))


def call(kernel, outs, scratch, flops, traffic, *args):
    return pl.pallas_call(
        kernel,
        out_shape=[jax.ShapeDtypeStruct(shape, kind) for shape, kind in outs],
        in_specs=[VMEM] * len(args),
        out_specs=[VMEM] * len(outs),
        scratch_shapes=[pltpu.VMEM(shape, kind) for shape, kind in scratch],
        compiler_params=pltpu.CompilerParams(vmem_limit_bytes=LIMIT),
        cost_estimate=pl.CostEstimate(flops=flops, bytes_accessed=traffic, transcendentals=0),
    )(*args)


def rows_of(store, step, first, length):
    ways = store.shape[0]
    pieces = []
    for turn in range(ways // step):
        row = first + step * turn
        pieces.append(store[row % ways, pl.ds(row // ways, length * step // ways)])
    return pieces


def put_rows(store, value, first, start, size):
    ways = store.shape[0]
    share = value.shape[0] // ways
    for turn in range(ways):
        row = first + turn
        store[row % ways, pl.ds(row // ways, share), :, start : start + size] = value[turn * share : (turn + 1) * share]


def clear_rows(store, rows):
    for row in rows:
        store[row % store.shape[0], row // store.shape[0]] = jnp.zeros(store.shape[2:], F32)


def flatten(pieces, start, size):
    return jnp.concatenate([p[:, :, start : start + size].reshape(-1, size) for p in pieces], 0).astype(BF16)


def turn_kernel(factor, source, top, rest):
    width = source.shape[0]
    skew = (source[...].T - source[...]) * factor
    first = halves(skew)
    two = dot3(first, first)
    square = halves(two)
    three = dot3(first, square)
    four = dot3(square, square)
    row = lax.broadcasted_iota(jnp.int32, (width, width), 0)
    eye = (row == lax.broadcasted_iota(jnp.int32, (width, width), 1)).astype(F32)
    upper = eye / 24.0 + skew / 120.0 + two / 720.0 + three / 5040.0 + four / 40320.0
    top[...], rest[...] = halves(skew + two / 2.0 + three / 6.0 + product(four, upper))


def encoder_kernel(*refs):
    far, raw, near = refs[:6], refs[6], refs[7:13]
    flat, lines, wide, one, two, arrived = refs[13:]
    copies = [pltpu.make_async_copy(far[k], near[k], arrived.at[k]) for k in range(6)]
    for copy in copies[:2]:
        copy.start()
    frames, kernel, second, third, observe, retain = near
    count, height, row = frames.shape
    lanes = lines.shape[3]
    wide[...] = jnp.zeros_like(wide)
    clear_rows(lines, (0, height + 1))
    clear_rows(one, (0, height // 2 + 1))
    clear_rows(two, (0, height // 4 + 1))
    edge = jnp.zeros(two.shape[:3] + (128,), F32)
    two[:, :, :, :128] = edge
    two[:, :, :, two.shape[3] - 128 :] = edge
    for copy in copies[:2]:
        copy.wait()
    for copy in copies[2:]:
        copy.start()
    pixels = frames[...].astype(F32).reshape(count * height, row)
    pixels = jnp.concatenate([pixels, jnp.zeros((count * height, lanes - row), F32)], 1)
    pixels = pltpu.roll(pixels, 9, 1)
    flat[0] = pixels[:, :128]
    flat[1] = pixels[:, 128:]
    for h in range(height):
        for side in range(2):
            picked = flat[side, pl.ds(h, count, stride=height), :]
            lines[(h + 1) % 8, (h + 1) // 8, :, 128 * side : 128 * side + 128] = picked
    taps, depth, broad = kernel.shape[0], 64, wide.shape[2]
    room = lanes - depth
    for tap in range(taps):
        colours = [kernel[tap, c].astype(F32) for c in range(3)]
        base = [colours[c][k : k + 1] for k in range(taps) for c in range(3)]
        base = jnp.concatenate(base + [jnp.zeros((depth - 12, 64), F32)], 0)
        band = jnp.concatenate([base] + [pltpu.roll(base, 6 * k, 0) for k in range(1, 8)], 1)
        wide[tap, room : room + depth, :] = band.astype(BF16)

    rows = height // 2
    sources = [flatten(rows_of(lines, 2, tap, rows), 0, lanes) for tap in range(taps)]
    halved = [[jnp.concatenate([p[:, k : k + 128] for p in sources[t : t + 2]], 1) for k in (0, 128)] for t in (0, 2)]
    total = one.shape[3]
    for start in range(0, total, broad):
        size = min(broad, total - start)
        shift = start // broad * 48
        value = None
        for side in range(2):
            if shift >= 128 * (side + 1) or shift + 54 <= 128 * side:
                continue
            first = room - shift + 128 * side
            for pair in range(2):
                weights = [wide[2 * pair + k, first : first + 128, :size] for k in range(2)]
                part = jnp.dot(halved[pair][side], jnp.concatenate(weights, 0), preferred_element_type=F32)
                value = part if value is None else value + part
        value = jnp.maximum(value, 0.0).astype(BF16).astype(F32)
        lane = lax.broadcasted_iota(jnp.int32, value.shape, 1) + start
        if start == 0:
            value = jnp.where(lane >= 64, value, 0.0)
        if start + size == total:
            value = jnp.where(lane < total - 64, value, 0.0)
        put_rows(one, value.reshape(rows, count, size), 1, start, size)

    copies[2].wait()
    rows = rows // 2
    weights = []
    for pair in range(2):
        taps_of = [second[2 * pair + k] for k in range(2)]
        sides = [jnp.concatenate([t[128 * side : 128 * side + 128] for t in taps_of], 0) for side in range(2)]
        weights.append(jnp.concatenate(sides, 1))
    left = None
    for tile in range(rows + 1):
        lanes_of = slice(128 * tile, 128 * tile + 128)
        value = None
        for pair in range(2):
            pieces = [flatten([p[:, :, lanes_of] for p in rows_of(one, 2, 2 * pair + k, rows)], 0, 128) for k in range(2)]
            part = jnp.dot(jnp.concatenate(pieces, 1), weights[pair], preferred_element_type=F32)
            value = part if value is None else value + part
        if tile > 0:
            result = jnp.maximum(left + value[:, 128:], 0.0).astype(BF16).astype(F32)
            put_rows(two, result.reshape(rows, count, 128), 1, 128 * tile, 128)
        left = value[:, :128]

    for copy in copies[3:]:
        copy.wait()
    rows = rows // 2
    value = jnp.zeros((rows * rows * count, third.shape[2]), F32)
    for tap in range(4):
        pieces = [flatten(rows_of(two, 2, tap, rows), 256 * j, 512) for j in range(rows)]
        value += jnp.dot(jnp.concatenate(pieces, 0), third[tap], preferred_element_type=F32)
    value = jnp.maximum(value, 0.0).reshape(rows * rows, count, value.shape[1])
    pooled = (jnp.sum(value, 0) * (1.0 / (rows * rows))).astype(BF16)
    raw[:count, :] = retain[...]
    raw[count:, :] = (1.0 - retain[...]) * jnp.dot(pooled, observe[...], preferred_element_type=F32)


def encode(frames, conv_first, second_kernel_weight, conv_third, observe_map, retain):
    count, height, row = frames.shape
    local, width = retain.shape
    far = [
        frames,
        jnp.transpose(conv_first, (0, 2, 1, 3)),
        second_kernel_weight.reshape(4, 256, 128),
        conv_third.reshape(4, 512, 256),
        observe_map,
        retain,
    ]
    scratch = [
        ((2, count * height, 128), F32),
        ((8, height // 8 + 1, count, 256), F32),
        ((4, 448, 512), BF16),
        ((4, height // 8 + 1, count, 34 * 64), F32),
        ((2, height // 8 + 1, count, 18 * 128), F32),
    ]
    return pl.pallas_call(
        encoder_kernel,
        out_shape=jax.ShapeDtypeStruct((2 * local, width), F32),
        in_specs=[pl.BlockSpec(memory_space=pltpu.HBM)] * len(far),
        out_specs=VMEM,
        scratch_shapes=[pltpu.VMEM(a.shape, a.dtype) for a in far]
        + [pltpu.VMEM(shape, kind) for shape, kind in scratch]
        + [pltpu.SemaphoreType.DMA((len(far),))],
        compiler_params=pltpu.CompilerParams(vmem_limit_bytes=60 * 1024 * 1024),
        cost_estimate=pl.CostEstimate(flops=5 * 10**9, bytes_accessed=2 * 10**6, transcendentals=0),
    )(*far)


def maps_kernel(mine, top, rest, raw, *refs):
    refs, place = refs[:-1], refs[-1]
    groups, count, rows, width = place.shape
    known, refs = (refs[:0], refs) if mine else (refs[: 3 - groups], refs[3 - groups :])
    local, spare = rows // 2, 16
    me = lax.axis_index("y")
    for group in range(groups):
        for slot in range(count):
            piece = raw[(group * count + slot) * rows : (group * count + slot + 1) * rows, :]
            place[group, pl.ds(lax.bitwise_xor(me, slot), 1)] = piece[None]
    turn = (top[...], rest[...])
    row = lax.broadcasted_iota(jnp.int32, (width, width), 0)
    eye = (row == lax.broadcasted_iota(jnp.int32, (width, width), 1)).astype(F32)
    start = eye + (turn[0].astype(F32) + turn[1].astype(F32))
    total = groups * count

    def line(block, step):
        return place[block // count, block % count, step : step + 1, :]

    def stack(step):
        lines = [line(block, step) for block in range(total)]
        return jnp.concatenate(lines + [jnp.zeros((spare - total, width), F32)], 0)

    values = [start * line(block, 0) for block in range(total)]
    states = stack(local)
    for step in range(1, local):
        both = jnp.concatenate([values[0], states], 0)
        both = both + dot3(halves(both), turn)
        states = both[width:] * stack(step) + stack(local + step)
        values[0] = both[:width] * line(0, step)
        for block in range(1, total):
            values[block] = (values[block] + dot3(halves(values[block]), turn)) * line(block, step)

    def spread(block):
        return jnp.broadcast_to(states[block : block + 1], (spare, width))

    results = []
    for group in range(groups):
        before = jnp.concatenate([values[group * count], spread(group * count)], 0)
        prefix = jnp.concatenate([eye, jnp.zeros((spare, width), F32)], 0)
        for k in range(1, count):
            block = group * count + k
            if mine:
                prefix = jnp.where(me == k, before, prefix)
            later = product(before, values[block])
            before = jnp.concatenate([later[:width], later[width:] + spread(block)], 0)
        results.append(before)
        if mine:
            refs[1][...] = prefix[: width + 8]
    if mine:
        refs[0][...] = results[0][: width + 8]
        return

    def joined(first, later):
        result = product(first, later[:width])
        return jnp.concatenate([result[:width], result[width:] + later[width:]], 0)

    z = lax.axis_index("z")
    odd, second = lax.rem(z, 2) == 1, lax.rem(z, 4) >= 2
    known = [jnp.concatenate([ref[...], ref[width:, :]], 0) for ref in known]
    if groups == 1:
        group, before = known
        other = results[0]
        refs[0][...] = joined(jnp.where(odd, other, group), jnp.where(odd, group, other))[: width + 8]
        refs[1][...] = jnp.where(odd, joined(other, before), before)[: width + 8]
        return
    pair = joined(*(jnp.where(odd, results[1 - k], results[k]) for k in range(2)))
    refs[0][...] = joined(jnp.where(second, pair, known[0]), jnp.where(second, known[0], pair))[: width + 8]
    refs[1][...] = pair[: width + 8]


def group_maps(mine, top, rest, raw, *known):
    width, groups = raw.shape[1], raw.shape[0] // 64
    outs = [((width + 8, width), F32)] * 2
    scratch = [((groups, 4, 16, width), F32)]
    cost = 4 * 10**9 * groups
    return call(functools.partial(maps_kernel, mine), outs, scratch, cost, 2 * 10**6, top, rest, raw, *known)


def ahead_kernel(top, rest, own, raw, maps_top, maps_rest, states):
    turn = (top[...], rest[...])
    width, local = own.shape[1], states.shape[0]
    value, state = own[:width, :], own[width:, :]
    for step in range(local):
        keep = raw[step : step + 1, :]
        value = (value + dot3(halves(value), turn)) * keep
        state = (state + dot3(halves(state), turn)) * keep + raw[local + step : local + step + 1, :]
        lanes = slice(step * width, (step + 1) * width)
        maps_top[:, lanes], maps_rest[:, lanes] = halves(value)
        states[step : step + 1, :] = state[0:1]


def final_kernel(entry, late, maps_top, maps_rest, states, out):
    width = states.shape[1]
    state = product(jnp.broadcast_to(entry[...], (8, width)), late[:width, :]) + late[width:, :]
    rows = dot3(halves(state), (maps_top[...], maps_rest[...]))
    for step in range(states.shape[0]):
        out[step : step + 1, :] = rows[0:1, step * width : (step + 1) * width] + states[step : step + 1, :]


def dot(a, b):
    return jnp.dot(a, b, precision=lax.Precision.HIGH, preferred_element_type=F32)


def exchange_pairs(bit, count):
    if 2 * bit == count:
        return [(i, count - 1 - i) for i in range(count)]
    return [(i, i ^ bit) for i in range(count)]


def join(low, high):
    width = low.shape[1]
    return dot(low, high[:width]) + jnp.concatenate([jnp.zeros((width, width), F32), high[width:]], 0)


def on_device(frames, conv_first, second_kernel_weight, conv_third, observe_map, skew_source, retain):
    local, width = retain.shape
    count_x, count_y, count_z = lax.axis_size("x"), lax.axis_size("y"), lax.axis_size("z")
    total_frames = local * count_x * count_y * count_z * lax.axis_size("core")
    me_x, me_z, me_core = lax.axis_index("x"), lax.axis_index("z"), lax.axis_index("core")
    factor = float(np.float32(0.7) / np.sqrt(np.float32(total_frames)))

    raw = encode(frames, conv_first, second_kernel_weight, conv_third, observe_map, retain)
    skew_source, raw = lax.optimization_barrier((skew_source, raw))
    square = ((width, width), BF16)
    top, rest = call(functools.partial(turn_kernel, factor), [square] * 2, [], 10**9, 10**6, skew_source)
    pieces = [lax.ppermute(raw, "y", [(i, i ^ k) for i in range(count_y)]) for k in range(1, count_y)]
    rows = jnp.concatenate([raw] + pieces, 0)
    beside = lax.ppermute(rows, "z", exchange_pairs(1, count_z))
    group, own = group_maps(True, top, rest, rows)
    beside, group = lax.optimization_barrier((beside, group))
    across = lax.ppermute(jnp.concatenate([rows, beside], 0), "z", exchange_pairs(2, count_z))
    pair, own = group_maps(False, top, rest, beside, group, own)
    across, pair = lax.optimization_barrier((across, pair))
    block, other_pair = group_maps(False, top, rest, across, pair)
    second = (me_z & 2) > 0

    other = lax.ppermute(block, "z", [(i, i ^ 6) for i in range(count_z)])
    own = jnp.where(second, join(other_pair, own), own)
    ahead = call(
        ahead_kernel,
        [((width, local * width), BF16)] * 2 + [((local, width), F32)],
        [],
        10**9,
        10**6,
        top,
        rest,
        own,
        raw,
    )
    other, *ahead = lax.optimization_barrier((other, *ahead))
    upper = (me_z & 4) > 0
    low_half = jnp.where(upper, other, block)
    block = join(low_half, jnp.where(upper, block, other))

    other = lax.ppermute(block, "core", exchange_pairs(1, 2))
    low_core, high_core = jnp.where(me_core > 0, other, block), jnp.where(me_core > 0, block, other)

    block = join(low_core, high_core)
    third = lax.ppermute(block, "x", [(2, 3)])
    block_end = block[width : width + 1]
    first_end = lax.ppermute(block_end, "x", [(0, 1)])
    still = jnp.concatenate([jnp.eye(width, dtype=F32), jnp.zeros((8, width), F32)], 0)
    late = join(jnp.where(me_core > 0, low_core, still), jnp.where(upper, low_half, still))
    first_end, late = lax.optimization_barrier((first_end, late))
    leaving = dot(first_end, block[:width]) + block_end
    for_fourth = lax.ppermute(leaving, "x", [(1, 3)])
    for_third = lax.ppermute(leaving, "x", [(1, 2)])
    entry = dot(for_fourth, third[:width]) + third[width : width + 1]
    for_third, entry = lax.optimization_barrier((for_third, entry))
    entry = jnp.where(me_x == 1, first_end, jnp.where(me_x == 2, for_third, entry))

    (filtered,) = call(
        final_kernel, [((local, width), F32)], [], 10**8, 10**6, entry, late, *ahead
    )
    return filtered


def solution(mesh):
    grp, seg = mesh.shape["grp"], mesh.shape["seg"]
    parts = Mesh(mesh.devices.reshape(grp // 2, 2, seg // 4, 4), ("x", "core", "z", "y"))
    whole = ("x", "core", "z", "y")
    placed = (P(whole), P(), P(), P(), P(), P(), P(whole))
    return jax.shard_map(on_device, mesh=parts, in_specs=placed, out_specs=P(whole), check_vma=False)
```

```python
import functools

import jax
import jax.numpy as jnp
import numpy as np
from jax import lax
from jax.experimental import pallas as pl
from jax.experimental.pallas import tpu as pltpu
from jax.sharding import Mesh, PartitionSpec as P

VMEM = pl.BlockSpec(memory_space=pltpu.VMEM)
LIMIT = 24 * 1024 * 1024
F32, BF16 = jnp.float32, jnp.bfloat16


def halves(value):
    top = value.astype(BF16)
    return top, (value - top.astype(F32)).astype(BF16)


def dot3(left, right):
    (left_top, left_rest), (right_top, right_rest) = left, right
    return (
        jnp.dot(left_top, right_rest, preferred_element_type=F32)
        + jnp.dot(left_rest, right_top, preferred_element_type=F32)
    ) + jnp.dot(left_top, right_top, preferred_element_type=F32)


def product(left, right):
    return dot3(halves(left), halves(right))


def call(kernel, outs, scratch, flops, traffic, *args):
    return pl.pallas_call(
        kernel,
        out_shape=[jax.ShapeDtypeStruct(shape, kind) for shape, kind in outs],
        in_specs=[VMEM] * len(args),
        out_specs=[VMEM] * len(outs),
        scratch_shapes=[pltpu.VMEM(shape, kind) for shape, kind in scratch],
        compiler_params=pltpu.CompilerParams(vmem_limit_bytes=LIMIT),
        cost_estimate=pl.CostEstimate(flops=flops, bytes_accessed=traffic, transcendentals=0),
    )(*args)


def rows_of(store, step, first, length):
    ways = store.shape[0]
    pieces = []
    for turn in range(ways // step):
        row = first + step * turn
        pieces.append(store[row % ways, pl.ds(row // ways, length * step // ways)])
    return pieces


def put_rows(store, value, first, start, size):
    ways = store.shape[0]
    share = value.shape[0] // ways
    for turn in range(ways):
        row = first + turn
        store[row % ways, pl.ds(row // ways, share), :, start : start + size] = value[turn * share : (turn + 1) * share]


def clear_rows(store, rows):
    for row in rows:
        store[row % store.shape[0], row // store.shape[0]] = jnp.zeros(store.shape[2:], F32)


def flatten(pieces, start, size):
    return jnp.concatenate([p[:, :, start : start + size].reshape(-1, size) for p in pieces], 0).astype(BF16)


def turn_kernel(factor, source, top, rest):
    width = source.shape[0]
    skew = (source[...].T - source[...]) * factor
    first = halves(skew)
    two = dot3(first, first)
    square = halves(two)
    three = dot3(first, square)
    four = dot3(square, square)
    row = lax.broadcasted_iota(jnp.int32, (width, width), 0)
    eye = (row == lax.broadcasted_iota(jnp.int32, (width, width), 1)).astype(F32)
    upper = eye / 24.0 + skew / 120.0 + two / 720.0 + three / 5040.0 + four / 40320.0
    top[...], rest[...] = halves(skew + two / 2.0 + three / 6.0 + product(four, upper))


def encoder_kernel(*refs):
    far, raw, near = refs[:6], refs[6], refs[7:13]
    flat, lines, wide, one, two, arrived = refs[13:]
    copies = [pltpu.make_async_copy(far[k], near[k], arrived.at[k]) for k in range(6)]
    for copy in copies[:2]:
        copy.start()
    frames, kernel, second, third, observe, retain = near
    count, height, row = frames.shape
    lanes = lines.shape[3]
    wide[...] = jnp.zeros_like(wide)
    clear_rows(lines, (0, height + 1))
    clear_rows(one, (0, height // 2 + 1))
    clear_rows(two, (0, height // 4 + 1))
    edge = jnp.zeros(two.shape[:3] + (128,), F32)
    two[:, :, :, :128] = edge
    two[:, :, :, two.shape[3] - 128 :] = edge
    for copy in copies[:2]:
        copy.wait()
    for copy in copies[2:]:
        copy.start()
    pixels = frames[...].astype(F32).reshape(count * height, row)
    pixels = jnp.concatenate([pixels, jnp.zeros((count * height, lanes - row), F32)], 1)
    pixels = pltpu.roll(pixels, 9, 1)
    flat[0] = pixels[:, :128]
    flat[1] = pixels[:, 128:]
    for h in range(height):
        for side in range(2):
            picked = flat[side, pl.ds(h, count, stride=height), :]
            lines[(h + 1) % 8, (h + 1) // 8, :, 128 * side : 128 * side + 128] = picked
    taps, depth, broad = kernel.shape[0], 64, wide.shape[2]
    room = lanes - depth
    for tap in range(taps):
        colours = [kernel[tap, c].astype(F32) for c in range(3)]
        base = [colours[c][k : k + 1] for k in range(taps) for c in range(3)]
        base = jnp.concatenate(base + [jnp.zeros((depth - 12, 64), F32)], 0)
        band = jnp.concatenate([base] + [pltpu.roll(base, 6 * k, 0) for k in range(1, 8)], 1)
        wide[tap, room : room + depth, :] = band.astype(BF16)

    rows = height // 2
    sources = [flatten(rows_of(lines, 2, tap, rows), 0, lanes) for tap in range(taps)]
    halved = [[jnp.concatenate([p[:, k : k + 128] for p in sources[t : t + 2]], 1) for k in (0, 128)] for t in (0, 2)]
    total = one.shape[3]
    for start in range(0, total, broad):
        size = min(broad, total - start)
        shift = start // broad * 48
        value = None
        for side in range(2):
            if shift >= 128 * (side + 1) or shift + 54 <= 128 * side:
                continue
            first = room - shift + 128 * side
            for pair in range(2):
                weights = [wide[2 * pair + k, first : first + 128, :size] for k in range(2)]
                part = jnp.dot(halved[pair][side], jnp.concatenate(weights, 0), preferred_element_type=F32)
                value = part if value is None else value + part
        value = jnp.maximum(value, 0.0).astype(BF16).astype(F32)
        lane = lax.broadcasted_iota(jnp.int32, value.shape, 1) + start
        if start == 0:
            value = jnp.where(lane >= 64, value, 0.0)
        if start + size == total:
            value = jnp.where(lane < total - 64, value, 0.0)
        put_rows(one, value.reshape(rows, count, size), 1, start, size)

    copies[2].wait()
    rows = rows // 2
    weights = []
    for pair in range(2):
        taps_of = [second[2 * pair + k] for k in range(2)]
        sides = [jnp.concatenate([t[128 * side : 128 * side + 128] for t in taps_of], 0) for side in range(2)]
        weights.append(jnp.concatenate(sides, 1))
    left = None
    for tile in range(rows + 1):
        lanes_of = slice(128 * tile, 128 * tile + 128)
        value = None
        for pair in range(2):
            pieces = [flatten([p[:, :, lanes_of] for p in rows_of(one, 2, 2 * pair + k, rows)], 0, 128) for k in range(2)]
            part = jnp.dot(jnp.concatenate(pieces, 1), weights[pair], preferred_element_type=F32)
            value = part if value is None else value + part
        if tile > 0:
            result = jnp.maximum(left + value[:, 128:], 0.0).astype(BF16).astype(F32)
            put_rows(two, result.reshape(rows, count, 128), 1, 128 * tile, 128)
        left = value[:, :128]

    for copy in copies[3:]:
        copy.wait()
    rows = rows // 2
    value = jnp.zeros((rows * rows * count, third.shape[2]), F32)
    for tap in range(4):
        pieces = [flatten(rows_of(two, 2, tap, rows), 256 * j, 512) for j in range(rows)]
        value += jnp.dot(jnp.concatenate(pieces, 0), third[tap], preferred_element_type=F32)
    value = jnp.maximum(value, 0.0).reshape(rows * rows, count, value.shape[1])
    pooled = (jnp.sum(value, 0) * (1.0 / (rows * rows))).astype(BF16)
    raw[:count, :] = retain[...]
    raw[count:, :] = (1.0 - retain[...]) * jnp.dot(pooled, observe[...], preferred_element_type=F32)


def encode(frames, conv_first, second_kernel_weight, conv_third, observe_map, retain):
    count, height, row = frames.shape
    local, width = retain.shape
    far = [
        frames,
        jnp.transpose(conv_first, (0, 2, 1, 3)),
        second_kernel_weight.reshape(4, 256, 128),
        conv_third.reshape(4, 512, 256),
        observe_map,
        retain,
    ]
    scratch = [
        ((2, count * height, 128), F32),
        ((8, height // 8 + 1, count, 256), F32),
        ((4, 448, 512), BF16),
        ((4, height // 8 + 1, count, 34 * 64), F32),
        ((2, height // 8 + 1, count, 18 * 128), F32),
    ]
    return pl.pallas_call(
        encoder_kernel,
        out_shape=jax.ShapeDtypeStruct((2 * local, width), F32),
        in_specs=[pl.BlockSpec(memory_space=pltpu.HBM)] * len(far),
        out_specs=VMEM,
        scratch_shapes=[pltpu.VMEM(a.shape, a.dtype) for a in far]
        + [pltpu.VMEM(shape, kind) for shape, kind in scratch]
        + [pltpu.SemaphoreType.DMA((len(far),))],
        compiler_params=pltpu.CompilerParams(vmem_limit_bytes=60 * 1024 * 1024),
        cost_estimate=pl.CostEstimate(flops=5 * 10**9, bytes_accessed=2 * 10**6, transcendentals=0),
    )(*far)


def maps_kernel(mine, top, rest, raw, *refs):
    refs, place = refs[:-1], refs[-1]
    groups, count, rows, width = place.shape
    known, refs = (refs[:0], refs) if mine else (refs[: 3 - groups], refs[3 - groups :])
    local, spare = rows // 2, 16
    me = lax.axis_index("y")
    for group in range(groups):
        for slot in range(count):
            piece = raw[(group * count + slot) * rows : (group * count + slot + 1) * rows, :]
            place[group, pl.ds(lax.bitwise_xor(me, slot), 1)] = piece[None]
    turn = (top[...], rest[...])
    row = lax.broadcasted_iota(jnp.int32, (width, width), 0)
    eye = (row == lax.broadcasted_iota(jnp.int32, (width, width), 1)).astype(F32)
    start = eye + (turn[0].astype(F32) + turn[1].astype(F32))
    total = groups * count

    def line(block, step):
        return place[block // count, block % count, step : step + 1, :]

    def stack(step):
        lines = [line(block, step) for block in range(total)]
        return jnp.concatenate(lines + [jnp.zeros((spare - total, width), F32)], 0)

    values = [start * line(block, 0) for block in range(total)]
    states = stack(local)
    for step in range(1, local):
        both = jnp.concatenate([values[0], states], 0)
        both = both + dot3(halves(both), turn)
        states = both[width:] * stack(step) + stack(local + step)
        values[0] = both[:width] * line(0, step)
        for block in range(1, total):
            values[block] = (values[block] + dot3(halves(values[block]), turn)) * line(block, step)

    def spread(block):
        return jnp.broadcast_to(states[block : block + 1], (spare, width))

    results = []
    for group in range(groups):
        before = jnp.concatenate([values[group * count], spread(group * count)], 0)
        prefix = jnp.concatenate([eye, jnp.zeros((spare, width), F32)], 0)
        for k in range(1, count):
            block = group * count + k
            if mine:
                prefix = jnp.where(me == k, before, prefix)
            later = product(before, values[block])
            before = jnp.concatenate([later[:width], later[width:] + spread(block)], 0)
        results.append(before)
        if mine:
            refs[1][...] = prefix[: width + 8]
    if mine:
        refs[0][...] = results[0][: width + 8]
        return

    def joined(first, later):
        result = product(first, later[:width])
        return jnp.concatenate([result[:width], result[width:] + later[width:]], 0)

    z = lax.axis_index("z")
    odd, second = lax.rem(z, 2) == 1, lax.rem(z, 4) >= 2
    known = [jnp.concatenate([ref[...], ref[width:, :]], 0) for ref in known]
    if groups == 1:
        group, before = known
        other = results[0]
        refs[0][...] = joined(jnp.where(odd, other, group), jnp.where(odd, group, other))[: width + 8]
        refs[1][...] = jnp.where(odd, joined(other, before), before)[: width + 8]
        return
    pair = joined(*(jnp.where(odd, results[1 - k], results[k]) for k in range(2)))
    refs[0][...] = joined(jnp.where(second, pair, known[0]), jnp.where(second, known[0], pair))[: width + 8]
    refs[1][...] = pair[: width + 8]


def group_maps(mine, top, rest, raw, *known):
    width, groups = raw.shape[1], raw.shape[0] // 64
    outs = [((width + 8, width), F32)] * 2
    scratch = [((groups, 4, 16, width), F32)]
    cost = 4 * 10**9 * groups
    return call(functools.partial(maps_kernel, mine), outs, scratch, cost, 2 * 10**6, top, rest, raw, *known)


def ahead_kernel(top, rest, own, raw, maps_top, maps_rest, states):
    turn = (top[...], rest[...])
    width, local = own.shape[1], states.shape[0]
    value, state = own[:width, :], own[width:, :]
    for step in range(local):
        keep = raw[step : step + 1, :]
        value = (value + dot3(halves(value), turn)) * keep
        state = (state + dot3(halves(state), turn)) * keep + raw[local + step : local + step + 1, :]
        lanes = slice(step * width, (step + 1) * width)
        maps_top[:, lanes], maps_rest[:, lanes] = halves(value)
        states[step : step + 1, :] = state[0:1]


def final_kernel(entry, late, maps_top, maps_rest, states, out):
    width = states.shape[1]
    state = product(jnp.broadcast_to(entry[...], (8, width)), late[:width, :]) + late[width:, :]
    rows = dot3(halves(state), (maps_top[...], maps_rest[...]))
    for step in range(states.shape[0]):
        out[step : step + 1, :] = rows[0:1, step * width : (step + 1) * width] + states[step : step + 1, :]


def dot(a, b):
    return jnp.dot(a, b, precision=lax.Precision.HIGH, preferred_element_type=F32)


def exchange_pairs(bit, count):
    if 2 * bit == count:
        return [(i, count - 1 - i) for i in range(count)]
    return [(i, i ^ bit) for i in range(count)]


def join(low, high):
    width = low.shape[1]
    return dot(low, high[:width]) + jnp.concatenate([jnp.zeros((width, width), F32), high[width:]], 0)


def on_device(frames, conv_first, second_kernel_weight, conv_third, observe_map, skew_source, retain):
    local, width = retain.shape
    count_x, count_y, count_z = lax.axis_size("x"), lax.axis_size("y"), lax.axis_size("z")
    total_frames = local * count_x * count_y * count_z * lax.axis_size("core")
    me_x, me_z, me_core = lax.axis_index("x"), lax.axis_index("z"), lax.axis_index("core")
    factor = float(np.float32(0.7) / np.sqrt(np.float32(total_frames)))

    raw = encode(frames, conv_first, second_kernel_weight, conv_third, observe_map, retain)
    skew_source, raw = lax.optimization_barrier((skew_source, raw))
    square = ((width, width), BF16)
    top, rest = call(functools.partial(turn_kernel, factor), [square] * 2, [], 10**9, 10**6, skew_source)
    pieces = [lax.ppermute(raw, "y", [(i, i ^ k) for i in range(count_y)]) for k in range(1, count_y)]
    rows = jnp.concatenate([raw] + pieces, 0)
    beside = lax.ppermute(rows, "z", exchange_pairs(1, count_z))
    group, own = group_maps(True, top, rest, rows)
    beside, group = lax.optimization_barrier((beside, group))
    across = lax.ppermute(jnp.concatenate([rows, beside], 0), "z", exchange_pairs(2, count_z))
    pair, own = group_maps(False, top, rest, beside, group, own)
    across, pair = lax.optimization_barrier((across, pair))
    block, other_pair = group_maps(False, top, rest, across, pair)
    second = (me_z & 2) > 0

    other = lax.ppermute(block, "z", [(i, i ^ 6) for i in range(count_z)])
    own = jnp.where(second, join(other_pair, own), own)
    ahead = call(
        ahead_kernel,
        [((width, local * width), BF16)] * 2 + [((local, width), F32)],
        [],
        10**9,
        10**6,
        top,
        rest,
        own,
        raw,
    )
    other, *ahead = lax.optimization_barrier((other, *ahead))
    upper = (me_z & 4) > 0
    low_half = jnp.where(upper, other, block)
    block = join(low_half, jnp.where(upper, block, other))

    other = lax.ppermute(block, "core", exchange_pairs(1, 2))
    low_core, high_core = jnp.where(me_core > 0, other, block), jnp.where(me_core > 0, block, other)
    block_end = dot(low_core[width : width + 1], high_core[:width]) + high_core[width : width + 1]
    block_end, low_core = lax.optimization_barrier((block_end, low_core))

    first_end = lax.ppermute(block_end, "x", [(i, i ^ 1) for i in range(count_x)])
    block = join(low_core, high_core)
    third = lax.ppermute(block, "x", [(2, 3)])
    still = jnp.concatenate([jnp.eye(width, dtype=F32), jnp.zeros((8, width), F32)], 0)
    late = join(jnp.where(me_core > 0, low_core, still), jnp.where(upper, low_half, still))
    first_end, late = lax.optimization_barrier((first_end, late))
    leaving = dot(first_end, block[:width]) + block_end
    for_fourth = lax.ppermute(leaving, "x", [(1, 3)])
    for_third = lax.ppermute(leaving, "x", [(1, 2)])
    entry = dot(for_fourth, third[:width]) + third[width : width + 1]
    for_third, entry = lax.optimization_barrier((for_third, entry))
    entry = jnp.where(me_x == 1, first_end, jnp.where(me_x == 2, for_third, entry))

    (filtered,) = call(
        final_kernel, [((local, width), F32)], [], 10**8, 10**6, entry, late, *ahead
    )
    return filtered


def solution(mesh):
    grp, seg = mesh.shape["grp"], mesh.shape["seg"]
    parts = Mesh(mesh.devices.reshape(grp // 2, 2, seg // 4, 4), ("x", "core", "z", "y"))
    whole = ("x", "core", "z", "y")
    placed = (P(whole), P(), P(), P(), P(), P(), P(whole))
    return jax.shard_map(on_device, mesh=parts, in_specs=placed, out_specs=P(whole), check_vma=False)
```
